128 devices in a mesh: resp: 8 (over x, core), head: 16 (over y, z).
Axes of the slice: x: 4, y: 4, z: 4, core: 2. Of those that a mesh axis runs over, the one named last changes fastest.
Arguments:
- queries: bfloat16 [8192, 24576], P('resp', 'head'), may hold values from -72 to 72
- up_key: bfloat16 [128, 128, 512], P('head'), may hold values from -0.5 to 0.5
- up_value: bfloat16 [128, 512, 128], P('head'), may hold values from -0.25 to 0.25
- prompt_latent: bfloat16 [16, 256, 576], P('resp', 'head'), may hold values from -8 to 8
- resp_latent: bfloat16 [8192, 576], P('resp'), may hold values from -6 to 6
- grad_out: bfloat16 [8192, 16384], P('resp', 'head'), may hold values from -6 to 6
- response_prompt: int32 [64], replicated, may hold values from 0 to 15, as said below
- prompt_length: int32 [16], replicated, may hold values from 1 to 256, 3072 in all
Outputs:
- attn_out: bfloat16 [8192, 16384], P('resp', 'head')
- prompt_grad: float32 [16, 256, 576], P('resp', 'head')
The draws below stay inside these ranges and needn't reach their ends.
Inputs may be any that keep to these rules, and one draw needn't show every extreme that they name: `response_prompt`: response n is held by index n // 8 of resp and prompt p is owned by index p // 2 of resp; the responses held by one index of resp never answer two different prompts of one owner.
All inputs are finite; a program needn't handle non-finite values.
Results may differ from the reference program's by a relative error of at most 0.013.
Values may be sent and summed in bfloat16 or wider, within the bound.
No kernel may reach another device: no remote copies, remote signals or barrier semaphores. Data moves between devices by JAX's collectives and lax.ppermute only.
A program may use at most 128 MiB of HBM per device.

```python
import math
import jax
import jax.numpy as jnp
import numpy as np
from jax import lax

HEADS = 128
NOPE = 128
ROPE = 64
LATENT = 512
VDIM = 128
PLEN = 256
RLEN = 128
RESP_DEV = 8
PROMPT_DEV = 2
NPROMPT = 16
NTOK = 8192
N_RESP = 8
N_HEAD = 16


def draw_queries(key, part):
    key = jax.random.fold_in(key, 11)
    key_one = jax.random.fold_in(key, 0)
    head_width = NOPE + ROPE
    drawn = jnp.clip(jax.random.normal(key_one, (NTOK, HEADS, head_width), jnp.float32), -6.0, 6.0)
    return drawn.reshape(NTOK, HEADS * head_width).astype(jnp.bfloat16)


def draw_prompt_latent(key, part):
    key = jax.random.fold_in(key, 12)
    key_one = jax.random.fold_in(key, 0)
    channels = LATENT + ROPE
    drawn = jnp.clip(jax.random.normal(key_one, (NPROMPT, PLEN, channels), jnp.float32), -6.0, 6.0)
    return drawn.astype(jnp.bfloat16)


def draw_response_prompt(key, part):
    key = jax.random.fold_in(key, 13)
    key_one, key_two, key_three = jax.random.split(key, 3)
    orders = jax.vmap(lambda subkey: jax.random.permutation(subkey, N_RESP))(jax.random.split(key_one, N_RESP))
    rank_index = jnp.broadcast_to((jnp.arange(RESP_DEV) % N_RESP)[None, :], (N_RESP, RESP_DEV))
    chosen = jax.random.randint(key_two, (N_RESP,), 0, min(RESP_DEV, N_RESP))
    rank_index = jnp.where(jnp.arange(RESP_DEV)[None, :] == RESP_DEV - 1, chosen[:, None], rank_index)
    owners = jnp.take_along_axis(orders, rank_index, axis=1)
    within = jax.random.randint(key_three, (N_RESP, N_RESP), 0, PROMPT_DEV)
    picked = jnp.take_along_axis(within, rank_index, axis=1)
    return (owners * PROMPT_DEV + picked).reshape(N_RESP * RESP_DEV).astype(jnp.int32)


def block_scale(own_key, extent, cuts, smallest, top_value):
    def one(dim, parts):
        steps = jax.random.uniform(jax.random.fold_in(jax.random.fold_in(own_key, 6), dim), (parts,), jnp.float32, smallest / len(cuts), top_value / len(cuts))
        return jnp.repeat(jnp.exp(steps), extent[dim] // parts).reshape((-1,) + (1,) * (len(extent) - dim - 1))

    gain = one(*cuts[0])
    for cut in cuts[1:]:
        gain = gain * one(*cut)
    return gain


def split_up(number_of, total, bound, slope):
    portions = [(1 << 20) // math.isqrt(rank ** slope) + 1 for rank in range(2, number_of + 1)]
    rest, holding = total - bound - (number_of - 1), [1] * (number_of - 1)
    while rest > 0:
        movable = [i for i in range(number_of - 1) if holding[i] < bound]
        pool, remaining = sum([portions[i] for i in movable]), rest
        for i in movable:
            addition = min(bound - holding[i], max(1, remaining * portions[i] // pool), rest)
            holding[i] = holding[i] + addition
            rest = rest - addition
    return np.array([bound] + holding)


def uneven(stream_key, count, total, most, lean):
    if count == 2:
        one = jax.random.randint(stream_key, (), max(1, total - most), min(most, total - 1) + 1)
        return jnp.stack([one, total - one])
    sizes = jnp.asarray(split_up(count, total, most, lean), jnp.int32)
    twos = (count - 1) // 2
    donor, sink = sizes[1:1 + 2 * twos:2], sizes[2:2 + 2 * twos:2]
    slack = jnp.minimum(donor - 1, most - sink)
    shifted = jax.random.randint(jax.random.fold_in(stream_key, 1), (twos,), 0, 1 << 20) % (slack + 1)
    sizes = sizes.at[1:1 + 2 * twos:2].set(donor - shifted).at[2:2 + 2 * twos:2].set(sink + shifted)
    return sizes[jax.random.permutation(jax.random.fold_in(stream_key, 2), count)]


def centred(rng, dims, spread, limit, cuts=(), dtype=jnp.bfloat16):
    level = block_scale(rng, dims, cuts, -0.22, 0.18) if cuts else 1.0
    entries = jax.random.normal(rng, dims, jnp.float32) * spread * level
    return jnp.minimum(jnp.maximum(entries, -limit), limit).astype(dtype)


def setup_inputs(seed: int = 0) -> dict:
    arg_keys = jax.random.split(jax.random.key(seed), 9)
    return {
        "queries": draw_queries(jax.random.fold_in(arg_keys[8], 71), 0),
        "up_key": centred(arg_keys[1], (HEADS, NOPE, LATENT), NOPE ** -0.5, 0.5, ((0, 16),)),
        "up_value": centred(arg_keys[2], (HEADS, LATENT, VDIM), LATENT ** -0.5, 0.25, ((0, 16),)),
        "prompt_latent": draw_prompt_latent(jax.random.fold_in(arg_keys[8], 71), 0),
        "resp_latent": centred(arg_keys[4], (NTOK, LATENT + ROPE), 1.0, 6.0, ((0, 8),)),
        "grad_out": centred(arg_keys[5], (NTOK, HEADS * VDIM), 1.0, 6.0, ((0, 8), (1, 16))),
        "response_prompt": draw_response_prompt(jax.random.fold_in(arg_keys[8], 71), 0),
        "prompt_length": uneven(arg_keys[7], NPROMPT, NPROMPT * PLEN * 3 // 4, PLEN, 2).astype(jnp.int32),
    }


def attend(queries, up_key, up_value, latent, length, own_rows, grad_out):
    nope_width = up_key.shape[1]
    latent_width = up_value.shape[1]
    row_count = queries.shape[0]
    key_span = latent.shape[0]
    scaling = 1.0 / math.sqrt(queries.shape[2])
    absorbed = jnp.einsum('lhn,hnc->lhc', queries[:, :, :nope_width].astype(jnp.float32), up_key.astype(jnp.float32)).astype(jnp.bfloat16)
    full_query = jnp.concatenate([absorbed, queries[:, :, nope_width:]], axis=2)
    key_rows = jnp.concatenate([latent, own_rows], axis=0)
    scores = jnp.einsum('lhc,kc->hlk', full_query.astype(jnp.float32), key_rows.astype(jnp.float32)) * scaling
    key_index = jnp.arange(key_span + row_count)
    row_index = jnp.arange(row_count)
    allowed = jnp.where(key_index[None, :] < key_span, key_index[None, :] < length, key_index[None, :] - key_span <= row_index[:, None])
    scores = jnp.where(allowed[None, :, :], scores, -jnp.inf)
    top_score = lax.optimization_barrier(jnp.max(scores, axis=2, keepdims=True))
    weights = jnp.exp(scores - top_score)
    attention = weights / lax.optimization_barrier(jnp.sum(weights, axis=2, keepdims=True))
    attention_low = attention.astype(jnp.bfloat16)
    values = key_rows[:, :latent_width]
    out_latent = jnp.einsum('hlk,kc->lhc', attention_low.astype(jnp.float32), values.astype(jnp.float32)).astype(jnp.bfloat16)
    result = jnp.einsum('lhc,hcv->lhv', out_latent.astype(jnp.float32), up_value.astype(jnp.float32)).astype(jnp.bfloat16)
    grad_latent = jnp.einsum('lhv,hcv->lhc', grad_out.astype(jnp.float32), up_value.astype(jnp.float32)).astype(jnp.bfloat16)
    grad_attention = jnp.einsum('lhc,kc->hlk', grad_latent.astype(jnp.float32), values.astype(jnp.float32))
    inner_sum = lax.optimization_barrier(jnp.sum(attention * grad_attention, axis=2, keepdims=True))
    grad_scores = (attention * (grad_attention - inner_sum) * scaling).astype(jnp.bfloat16)
    key_term = jnp.einsum('hlk,lhc->kc', grad_scores[:, :, :key_span].astype(jnp.float32), full_query.astype(jnp.float32))
    value_term = jnp.einsum('hlk,lhc->kc', attention_low[:, :, :key_span].astype(jnp.float32), grad_latent.astype(jnp.float32))
    combined = key_term + jnp.pad(value_term, ((0, 0), (0, key_term.shape[1] - latent_width)))
    return (result, combined)

def reference(queries, up_key, up_value, prompt_latent, resp_latent, grad_out, response_prompt, prompt_length):
    shaped_query = queries.reshape(N_RESP, RESP_DEV, RLEN, N_HEAD, HEADS // N_HEAD, NOPE + ROPE)
    shaped_grad = grad_out.reshape(N_RESP, RESP_DEV, RLEN, N_HEAD, HEADS // N_HEAD, VDIM)
    shaped_own = resp_latent.reshape(N_RESP, RESP_DEV, RLEN, LATENT + ROPE)
    owner_prompts = response_prompt.reshape(N_RESP, RESP_DEV)
    key_up = up_key.reshape(N_HEAD, HEADS // N_HEAD, NOPE, LATENT)
    value_up = up_value.reshape(N_HEAD, HEADS // N_HEAD, LATENT, VDIM)

    def one_response(inputs):
        group_query, own_rows, group_grad, prompt_id = inputs
        latent = lax.dynamic_index_in_dim(prompt_latent, prompt_id, 0, False)
        length = lax.dynamic_index_in_dim(prompt_length, prompt_id, 0, False)

        def one_group(pieces):
            return attend(pieces[0], pieces[1], pieces[2], latent, length, own_rows, pieces[3])
        return lax.map(one_group, (jnp.moveaxis(group_query, 1, 0), key_up, value_up, jnp.moveaxis(group_grad, 1, 0)))

    def one_device(running, inputs):
        dev_query, dev_own, dev_grad, dev_prompt = inputs
        outputs, term_stack = lax.map(one_response, (dev_query, dev_own, dev_grad, dev_prompt))
        same_prompt = dev_prompt[:, None] == dev_prompt[None, :]
        slot_order = jnp.arange(RESP_DEV)
        leading = jnp.logical_not(jnp.any(same_prompt & (slot_order[None, :] < slot_order[:, None]), axis=1))
        partial_value = jnp.einsum('jk,kgsc->jgsc', same_prompt.astype(jnp.float32), term_stack, precision=lax.Precision.HIGHEST)
        rounded = lax.optimization_barrier(partial_value.astype(jnp.bfloat16)).astype(jnp.float32)
        summed = lax.optimization_barrier(jnp.sum(rounded, axis=1)) * leading.astype(jnp.float32)[:, None, None]
        for slot_index in range(RESP_DEV):
            running = running.at[dev_prompt[slot_index]].add(summed[slot_index])
        return (running, outputs)
    zero_grad = jnp.zeros((NPROMPT, PLEN, LATENT + ROPE), jnp.float32)
    prompt_grad, stacked = lax.scan(one_device, zero_grad, (shaped_query, shaped_own, shaped_grad, owner_prompts))
    attn_out = jnp.transpose(stacked, (0, 1, 3, 2, 4, 5)).reshape(NTOK, HEADS * VDIM)
    return (attn_out, prompt_grad)
```

```python
import functools
import math

import jax
import jax.numpy as jnp
from jax import lax
from jax.experimental import pallas as pl
from jax.experimental.pallas import tpu as pltpu
from jax.sharding import PartitionSpec as P

BF16 = jnp.bfloat16
F32 = jnp.float32
VMEM_LIMIT = 60 * 1024 * 1024
LOG2E = 1.4426950408889634


def dot_nn(a, b):
    return lax.dot_general(a, b, (((1,), (0,)), ((), ())), preferred_element_type=F32)


def dot_nt(a, b):
    return lax.dot_general(a, b, (((1,), (1,)), ((), ())), preferred_element_type=F32)


def up_kernel(q_ref, uk_ref, go_ref, uv_ref, fq_ref, gl_ref):
    resp_count, channels, _ = fq_ref.shape
    latent_width = gl_ref.shape[1]
    rope = channels - latent_width
    rows = q_ref.shape[0] // resp_count
    nope = uk_ref.shape[1]
    span = 2 * nope
    for e in range(2):
        lead = e * rope
        lift = uk_ref[e]
        parts = [lift, jnp.zeros((nope - lead, latent_width), BF16)]
        if lead:
            parts = [jnp.zeros((lead, latent_width), BF16)] + parts
        lifted = jnp.concatenate(parts, axis=0).T
        row = lax.broadcasted_iota(jnp.int32, (rope, span), 0)
        col = lax.broadcasted_iota(jnp.int32, (rope, span), 1)
        pick = jnp.where(col == row + (nope + lead), 1.0, 0.0).astype(BF16)
        up_value = uv_ref[e]
        for j in range(0, resp_count, 2):
            window = q_ref[pl.ds(j * rows, 2 * rows), pl.ds(e * nope, span)]
            grad = go_ref[pl.ds(j * rows, 2 * rows), pl.ds(e * rows, rows)]
            top = dot_nt(lifted, window).astype(BF16)
            low = dot_nt(pick, window).astype(BF16)
            lat = dot_nt(up_value, grad).astype(BF16)
            for i in range(2):
                src = slice(i * rows, (i + 1) * rows)
                dst = pl.ds(e * rows, rows)
                fq_ref[j + i, pl.ds(0, latent_width), dst] = top[:, src]
                fq_ref[j + i, pl.ds(latent_width, rope), dst] = low[:, src]
                gl_ref[j + i, :, dst] = lat[:, src]


def lift_tokens(queries, up_key, grad_out, up_value, resp_count):
    tokens = queries.shape[0]
    rows = tokens // resp_count
    heads, nope, latent_width = up_key.shape
    value_width = up_value.shape[2]
    head_width = queries.shape[1] // heads
    channels = latent_width + head_width - nope
    return pl.pallas_call(
        up_kernel,
        grid=(heads // 2,),
        in_specs=[
            pl.BlockSpec((tokens, 2 * head_width), lambda i: (0, i)),
            pl.BlockSpec((2, nope, latent_width), lambda i: (i, 0, 0)),
            pl.BlockSpec((tokens, 2 * value_width), lambda i: (0, i)),
            pl.BlockSpec((2, latent_width, value_width), lambda i: (i, 0, 0)),
        ],
        out_specs=[
            pl.BlockSpec((resp_count, channels, 2 * rows), lambda i: (0, 0, i)),
            pl.BlockSpec((resp_count, latent_width, 2 * rows), lambda i: (0, 0, i)),
        ],
        out_shape=[
            jax.ShapeDtypeStruct((resp_count, channels, heads * rows), BF16),
            jax.ShapeDtypeStruct((resp_count, latent_width, heads * rows), BF16),
        ],
        compiler_params=pltpu.CompilerParams(vmem_limit_bytes=VMEM_LIMIT),
        cost_estimate=pl.CostEstimate(
            flops=4 * tokens * heads * nope * latent_width,
            bytes_accessed=30 * 1024 * 1024,
            transcendentals=0,
        ),
        name="lift_tokens",
    )(queries, up_key, grad_out, up_value)


def attend_kernel(
    head_width, slot_ref, len_ref, latent_ref, own_ref, fq_ref, gl_ref, aT_ref, piece_ref, acc_ref, gs_ref
):
    j = pl.program_id(0)
    steps = pl.num_programs(0)
    key_span = latent_ref.shape[1]
    rows = own_ref.shape[0]
    channels = own_ref.shape[1]
    latent_width = gl_ref.shape[1]
    columns = fq_ref.shape[2]
    rope = channels - latent_width
    scaling = 1.0 / math.sqrt(head_width)
    chunk = 2 * rows

    @pl.when(j == 0)
    def _():
        acc_ref[...] = jnp.zeros_like(acc_ref)

    length = len_ref[j]
    keys = jnp.concatenate([latent_ref[0], own_ref[...]], axis=0)
    values = keys[:, :latent_width]
    row = lax.broadcasted_iota(jnp.int32, (key_span + rows, chunk), 0)
    col = lax.broadcasted_iota(jnp.int32, (key_span + rows, chunk), 1) % rows
    bound = jnp.where(row < key_span, length, col + (key_span + 1))
    allowed = row < bound
    for c in range(columns // chunk):
        at = pl.ds(c * chunk, chunk)
        scores = dot_nn(keys, fq_ref[0, :, at])
        grad_att = dot_nn(values, gl_ref[0, :, at])
        scores = jnp.where(allowed, scores * (scaling * LOG2E), -1e30)
        top = jnp.max(scores, axis=0, keepdims=True)
        weights = jnp.exp2(scores - top)
        total = jnp.sum(weights, axis=0, keepdims=True)
        attention = weights * (1.0 / total)
        inner = jnp.sum(attention * grad_att, axis=0, keepdims=True)
        aT_ref[0, :, at] = attention.astype(BF16)
        grad_scores = attention[:key_span] * ((grad_att[:key_span] - inner) * scaling)
        gs_ref[:, at] = grad_scores.astype(BF16)
    combined = dot_nt(gs_ref[...], fq_ref[0])
    value_term = dot_nt(aT_ref[0, pl.ds(0, key_span), :], gl_ref[0])
    slot = slot_ref[j]
    acc_ref[slot, :, pl.ds(0, latent_width)] += combined[:, :latent_width] + value_term
    acc_ref[slot, :, pl.ds(latent_width, rope)] += combined[:, latent_width:]

    @pl.when(j == steps - 1)
    def _():
        piece_ref[...] = acc_ref[...].astype(BF16)


def attend(slots, lengths, gathered, resp_latent, full_t, grad_t, head_width):
    groups, key_span, channels = gathered.shape
    resp_count, _, columns = full_t.shape
    latent_width = grad_t.shape[1]
    rows = resp_latent.shape[0] // resp_count
    grid_spec = pltpu.PrefetchScalarGridSpec(
        num_scalar_prefetch=2,
        grid=(resp_count,),
        in_specs=[
            pl.BlockSpec((1, key_span, channels), lambda j, s, n: (s[j], 0, 0)),
            pl.BlockSpec((rows, channels), lambda j, s, n: (j, 0)),
            pl.BlockSpec((1, channels, columns), lambda j, s, n: (j, 0, 0)),
            pl.BlockSpec((1, latent_width, columns), lambda j, s, n: (j, 0, 0)),
        ],
        out_specs=[
            pl.BlockSpec((1, key_span + rows, columns), lambda j, s, n: (j, 0, 0)),
            pl.BlockSpec((groups, key_span, channels), lambda j, s, n: (0, 0, 0)),
        ],
        scratch_shapes=[
            pltpu.VMEM((groups, key_span, channels), F32),
            pltpu.VMEM((key_span, columns), BF16),
        ],
    )
    return pl.pallas_call(
        functools.partial(attend_kernel, head_width),
        grid_spec=grid_spec,
        out_shape=[
            jax.ShapeDtypeStruct((resp_count, key_span + rows, columns), BF16),
            jax.ShapeDtypeStruct((groups, key_span, channels), BF16),
        ],
        compiler_params=pltpu.CompilerParams(vmem_limit_bytes=VMEM_LIMIT),
        cost_estimate=pl.CostEstimate(
            flops=2 * resp_count * columns * 384 * 2200,
            bytes_accessed=30 * 1024 * 1024,
            transcendentals=resp_count * columns * 384,
        ),
        name="attend",
    )(slots, lengths, gathered, resp_latent, full_t, grad_t)


def output_kernel(slot_ref, latent_ref, own_ref, aT_ref, uv_ref, out_ref):
    rows = own_ref.shape[0]
    heads, latent_width, value_width = uv_ref.shape
    values = jnp.concatenate(
        [latent_ref[0, :, pl.ds(0, latent_width)], own_ref[:, pl.ds(0, latent_width)]], axis=0
    )
    values_t = values.T
    for i in range(0, heads, 2):
        at = pl.ds(i * rows, 2 * rows)
        latent_t = dot_nn(values_t, aT_ref[0, :, at]).astype(BF16)
        for e in range(2):
            part = latent_t[:, e * rows : (e + 1) * rows].T
            done = dot_nn(part, uv_ref[i + e])
            out_ref[:, pl.ds((i + e) * value_width, value_width)] = done.astype(BF16)


def outputs(slots, gathered, resp_latent, attention_t, up_value):
    groups, key_span, channels = gathered.shape
    resp_count, keys, columns = attention_t.shape
    heads, latent_width, value_width = up_value.shape
    rows = resp_latent.shape[0] // resp_count
    grid_spec = pltpu.PrefetchScalarGridSpec(
        num_scalar_prefetch=1,
        grid=(resp_count,),
        in_specs=[
            pl.BlockSpec((1, key_span, channels), lambda j, s: (s[j], 0, 0)),
            pl.BlockSpec((rows, channels), lambda j, s: (j, 0)),
            pl.BlockSpec((1, keys, columns), lambda j, s: (j, 0, 0)),
            pl.BlockSpec((heads, latent_width, value_width), lambda j, s: (0, 0, 0)),
        ],
        out_specs=pl.BlockSpec((rows, heads * value_width), lambda j, s: (j, 0)),
    )
    return pl.pallas_call(
        output_kernel,
        grid_spec=grid_spec,
        out_shape=jax.ShapeDtypeStruct((resp_count * rows, heads * value_width), BF16),
        compiler_params=pltpu.CompilerParams(vmem_limit_bytes=VMEM_LIMIT),
        cost_estimate=pl.CostEstimate(
            flops=2 * resp_count * columns * (384 + 128) * 512,
            bytes_accessed=16 * 1024 * 1024,
            transcendentals=0,
        ),
        name="outputs",
    )(slots, gathered, resp_latent, attention_t, up_value)


def on_device(
    queries, up_key, up_value, prompt_latent, resp_latent, grad_out, response_prompt, prompt_length
):
    groups = lax.axis_size("resp")
    slab_count = lax.axis_size("head")
    my_group = lax.axis_index("resp")
    owned, slab_rows, channels = prompt_latent.shape
    key_span = slab_rows * slab_count
    resp_count = response_prompt.shape[0] // groups
    owners = response_prompt // owned
    hit_table = owners[:, None] == jnp.arange(groups)[None, :]
    wanted = jnp.max(
        jnp.where(hit_table, (response_prompt % owned)[:, None], -1).reshape(
            groups, resp_count, groups
        ),
        axis=1,
    )
    wanted_mine = lax.dynamic_index_in_dim(wanted, my_group, 1, False)
    outgoing = jnp.where(
        (wanted_mine == 1)[:, None, None], prompt_latent[1][None], prompt_latent[0][None]
    )
    copies = jnp.repeat(outgoing, slab_count, axis=0)
    arrived = lax.all_to_all(copies, ("resp", "head"), split_axis=0, concat_axis=0, tiled=True)
    gathered = arrived.reshape(groups, key_span, channels)
    local_prompt = lax.dynamic_slice_in_dim(response_prompt, my_group * resp_count, resp_count)
    slots = local_prompt // owned
    hits = local_prompt[:, None] == jnp.arange(prompt_length.shape[0])[None, :]
    lengths = jnp.sum(jnp.where(hits, prompt_length[None, :], 0), axis=1)
    full_t, grad_t = lift_tokens(queries, up_key, grad_out, up_value, resp_count)
    attention_t, pieces = attend(slots, lengths, gathered, resp_latent, full_t, grad_t, queries.shape[1] // up_key.shape[0])
    returned_grad = lax.all_to_all(
        pieces.reshape(groups * slab_count, slab_rows, channels),
        ("resp", "head"),
        split_axis=0,
        concat_axis=0,
        tiled=True,
    )
    attn_out = outputs(slots, gathered, resp_latent, attention_t, up_value)
    summed = jnp.sum(
        returned_grad.reshape(groups, slab_count, slab_rows, channels).astype(F32), axis=1
    )
    prompt_grad = jnp.stack(
        [
            jnp.sum(jnp.where((wanted_mine == p)[:, None, None], summed, 0.0), axis=0)
            for p in range(owned)
        ]
    )
    return (attn_out, prompt_grad)


def solution(mesh):
    return jax.shard_map(
        on_device,
        mesh=mesh,
        in_specs=(
            P("resp", "head"),
            P("head", None, None),
            P("head", None, None),
            P("resp", "head", None),
            P("resp", None),
            P("resp", "head"),
            P(),
            P(),
        ),
        out_specs=(P("resp", "head"), P("resp", "head", None)),
        check_vma=False,
    )
```

```python
import functools
import math

import jax
import jax.numpy as jnp
from jax import lax
from jax.experimental import pallas as pl
from jax.experimental.pallas import tpu as pltpu
from jax.sharding import PartitionSpec as P

BF16 = jnp.bfloat16
F32 = jnp.float32
LOG2E = 1.4426950408889634


def dot_nn(a, b):
    return lax.dot_general(a, b, (((1,), (0,)), ((), ())), preferred_element_type=F32)


def dot_nt(a, b):
    return lax.dot_general(a, b, (((1,), (1,)), ((), ())), preferred_element_type=F32)


def up_kernel(q_ref, uk_ref, go_ref, uv_ref, fq_ref, gl_ref):
    resp_count, channels, _ = fq_ref.shape
    latent_width = gl_ref.shape[1]
    rope = channels - latent_width
    rows = q_ref.shape[0] // resp_count
    nope = uk_ref.shape[1]
    span = 2 * nope
    for e in range(2):
        lead = e * rope
        lift = uk_ref[e]
        parts = [lift, jnp.zeros((nope - lead, latent_width), BF16)]
        if lead:
            parts = [jnp.zeros((lead, latent_width), BF16)] + parts
        lifted = jnp.concatenate(parts, axis=0).T
        row = lax.broadcasted_iota(jnp.int32, (rope, span), 0)
        col = lax.broadcasted_iota(jnp.int32, (rope, span), 1)
        pick = jnp.where(col == row + (nope + lead), 1.0, 0.0).astype(BF16)
        up_value = uv_ref[e]
        for j in range(0, resp_count, 2):
            window = q_ref[pl.ds(j * rows, 2 * rows), pl.ds(e * nope, span)]
            grad = go_ref[pl.ds(j * rows, 2 * rows), pl.ds(e * rows, rows)]
            top = dot_nt(lifted, window).astype(BF16)
            low = dot_nt(pick, window).astype(BF16)
            lat = dot_nt(up_value, grad).astype(BF16)
            for i in range(2):
                src = slice(i * rows, (i + 1) * rows)
                dst = pl.ds(e * rows, rows)
                fq_ref[j + i, pl.ds(0, latent_width), dst] = top[:, src]
                fq_ref[j + i, pl.ds(latent_width, rope), dst] = low[:, src]
                gl_ref[j + i, :, dst] = lat[:, src]


def lift_tokens(queries, up_key, grad_out, up_value, resp_count):
    tokens = queries.shape[0]
    rows = tokens // resp_count
    heads, nope, latent_width = up_key.shape
    value_width = up_value.shape[2]
    head_width = queries.shape[1] // heads
    channels = latent_width + head_width - nope
    return pl.pallas_call(
        up_kernel,
        grid=(heads // 2,),
        in_specs=[
            pl.BlockSpec((tokens, 2 * head_width), lambda i: (0, i)),
            pl.BlockSpec((2, nope, latent_width), lambda i: (i, 0, 0)),
            pl.BlockSpec((tokens, 2 * value_width), lambda i: (0, i)),
            pl.BlockSpec((2, latent_width, value_width), lambda i: (i, 0, 0)),
        ],
        out_specs=[
            pl.BlockSpec((resp_count, channels, 2 * rows), lambda i: (0, 0, i)),
            pl.BlockSpec((resp_count, latent_width, 2 * rows), lambda i: (0, 0, i)),
        ],
        out_shape=[
            jax.ShapeDtypeStruct((resp_count, channels, heads * rows), BF16),
            jax.ShapeDtypeStruct((resp_count, latent_width, heads * rows), BF16),
        ],
        compiler_params=pltpu.CompilerParams(vmem_limit_bytes=14*1024*1024),
        cost_estimate=pl.CostEstimate(
            flops=4 * tokens * heads * nope * latent_width,
            bytes_accessed=30 * 1024 * 1024,
            transcendentals=0,
        ),
        name="lift_tokens",
    )(queries, up_key, grad_out, up_value)


def pack_rows(rows):
    slab, channels = rows.shape
    blocks = channels // 128
    half = slab // 2
    tail = jnp.concatenate([rows[:half, 128 * blocks :], rows[half:, 128 * blocks :]], axis=1)
    return jnp.concatenate([rows[:, 128 * c : 128 * (c + 1)] for c in range(blocks)] + [tail], axis=0)


def pack_kernel(prompt_ref, group_ref, latent_ref, out_ref):
    groups, slab_count, packed_rows, lanes = out_ref.shape
    owned = latent_ref.shape[0]
    resp_count = prompt_ref.shape[0] // groups
    packed = [pack_rows(latent_ref[p].astype(F32)) for p in range(owned)]
    for r in range(groups):
        wanted = jnp.int32(-1)
        for i in range(resp_count):
            prompt = prompt_ref[r * resp_count + i]
            wanted = jnp.where(prompt // owned == group_ref[0], prompt % owned, wanted)
        chosen = packed[0]
        for p in range(1, owned):
            chosen = jnp.where(wanted == p, packed[p], chosen)
        chosen = chosen.astype(BF16)
        out_ref[r] = jnp.broadcast_to(chosen[None], (slab_count, packed_rows, lanes))


def pack(response_prompt, my_group, prompt_latent, groups, slab_count):
    owned, slab_rows, channels = prompt_latent.shape
    packed_rows = slab_rows * channels // 128
    return pl.pallas_call(
        pack_kernel,
        grid_spec=pltpu.PrefetchScalarGridSpec(
            num_scalar_prefetch=2,
            grid=(1,),
            in_specs=[pl.BlockSpec((owned, slab_rows, channels), lambda i, p, g: (0, 0, 0))],
            out_specs=pl.BlockSpec(
                (groups, slab_count, packed_rows, 128), lambda i, p, g: (0, 0, 0, 0)
            ),
        ),
        out_shape=jax.ShapeDtypeStruct((groups, slab_count, packed_rows, 128), BF16),
        compiler_params=pltpu.CompilerParams(vmem_limit_bytes=10 * 1024 * 1024),
        name="pack",
    )(response_prompt, my_group, prompt_latent)


def own_kernel(head_width, own_ref, fq_ref, gl_ref, e_ref, stat_ref):
    rows = own_ref.shape[0]
    latent_width = gl_ref.shape[1]
    columns = fq_ref.shape[2]
    scaling = LOG2E / math.sqrt(head_width)
    chunk = 2 * rows
    keys = own_ref[...]
    values = keys[:, :latent_width]
    row = lax.broadcasted_iota(jnp.int32, (rows, chunk), 0)
    col = lax.broadcasted_iota(jnp.int32, (rows, chunk), 1) % rows
    allowed = row <= col
    for c in range(columns // chunk):
        at = pl.ds(c * chunk, chunk)
        scores = dot_nn(keys, fq_ref[0, :, at])
        grad_att = dot_nn(values, gl_ref[0, :, at])
        scores = jnp.where(allowed, scores * scaling, -1e30)
        top = jnp.max(scores, axis=0, keepdims=True)
        weights = jnp.exp2(scores - top)
        e_ref[0, :, at] = weights.astype(BF16)
        stat_ref[0, pl.ds(0, 1), at] = top
        stat_ref[0, pl.ds(1, 1), at] = jnp.sum(weights, axis=0, keepdims=True)
        stat_ref[0, pl.ds(2, 1), at] = jnp.sum(weights * grad_att, axis=0, keepdims=True)


def own_scores(resp_latent, full_t, grad_t, head_width):
    resp_count, channels, columns = full_t.shape
    latent_width = grad_t.shape[1]
    rows = resp_latent.shape[0] // resp_count
    return pl.pallas_call(
        functools.partial(own_kernel, head_width),
        grid=(resp_count,),
        in_specs=[
            pl.BlockSpec((rows, channels), lambda j: (j, 0)),
            pl.BlockSpec((1, channels, columns), lambda j: (j, 0, 0)),
            pl.BlockSpec((1, latent_width, columns), lambda j: (j, 0, 0)),
        ],
        out_specs=[
            pl.BlockSpec((1, rows, columns), lambda j: (j, 0, 0)),
            pl.BlockSpec((1, 8, columns), lambda j: (j, 0, 0)),
        ],
        out_shape=[
            jax.ShapeDtypeStruct((resp_count, rows, columns), BF16),
            jax.ShapeDtypeStruct((resp_count, 8, columns), F32),
        ],
        compiler_params=pltpu.CompilerParams(vmem_limit_bytes=10*1024*1024),
        cost_estimate=pl.CostEstimate(
            flops=2 * resp_count * columns * rows * (channels + latent_width),
            bytes_accessed=22 * 1024 * 1024,
            transcendentals=resp_count * columns * rows,
        ),
        name="own_scores",
    )(resp_latent, full_t, grad_t)


def unpack_latent(packed_ref, slab):
    slabs, packed_rows, lanes = packed_ref.shape[1:]
    return jnp.concatenate(
        [
            jnp.concatenate(
                [packed_ref[0, h, pl.ds(slab * c, slab), :] for h in range(slabs)], axis=0
            )
            for c in range(packed_rows // slab)
        ],
        axis=1,
    )


def unpack_rope(packed_ref, slab):
    slabs, packed_rows, lanes = packed_ref.shape[1:]
    rows = []
    for h in range(slabs):
        tail = packed_ref[0, h].astype(F32)[packed_rows - slab // 2 :]
        rows += [tail[:, : lanes // 2], tail[:, lanes // 2 :]]
    return jnp.concatenate(rows, axis=0).astype(BF16)


def attend_kernel(
    head_width,
    slot_ref,
    len_ref,
    latent_ref,
    stat_ref,
    fq_ref,
    gl_ref,
    aT_ref,
    ratio_ref,
    piece_ref,
    acc_ref,
    gs_ref,
):
    j = pl.program_id(0)
    steps = pl.num_programs(0)
    channels = fq_ref.shape[1]
    latent_width = gl_ref.shape[1]
    columns = fq_ref.shape[2]
    rope = channels - latent_width
    groups, key_span, _ = acc_ref.shape
    slabs = latent_ref.shape[1]
    slab = key_span // slabs
    scaling = 1.0 / math.sqrt(head_width)
    chunk = 256

    @pl.when(j == 0)
    def _():
        acc_ref[...] = jnp.zeros_like(acc_ref)

    length = len_ref[j]
    values = unpack_latent(latent_ref, slab)
    keys = jnp.concatenate([values, unpack_rope(latent_ref, slab)], axis=1)
    row = lax.broadcasted_iota(jnp.int32, (key_span, chunk), 0)
    allowed = row < length
    for c in range(columns // chunk):
        at = pl.ds(c * chunk, chunk)
        scores = dot_nn(keys, fq_ref[0, :, at])
        grad_att = dot_nn(values, gl_ref[0, :, at])
        own_top = stat_ref[0, pl.ds(0, 1), at]
        scores = jnp.where(allowed, scores * (scaling * LOG2E), -1e30)
        top = jnp.maximum(jnp.max(scores, axis=0, keepdims=True), own_top)
        weights = jnp.exp2(scores - top)
        shift = jnp.exp2(own_top - top)
        total = jnp.sum(weights, axis=0, keepdims=True) + shift * stat_ref[0, pl.ds(1, 1), at]
        inverse = 1.0 / total
        inner = jnp.sum(weights * grad_att, axis=0, keepdims=True)
        inner = (inner + shift * stat_ref[0, pl.ds(2, 1), at]) * inverse
        attention = weights * inverse
        aT_ref[0, :, at] = attention.astype(BF16)
        gs_ref[:, at] = (attention * ((grad_att - inner) * scaling)).astype(BF16)
        ratio_ref[0, pl.ds(0, 1), at] = shift * inverse
    combined = dot_nt(gs_ref[...], fq_ref[0])
    value_term = dot_nt(aT_ref[0], gl_ref[0])
    slot = slot_ref[j]
    acc_ref[slot, :, pl.ds(0, latent_width)] += combined[:, :latent_width] + value_term
    acc_ref[slot, :, pl.ds(latent_width, rope)] += combined[:, latent_width:]

    @pl.when(j == steps - 1)
    def _():
        for g in range(groups):
            for h in range(slabs):
                rows = acc_ref[g, pl.ds(h * slab, slab), :]
                piece_ref[g, h] = pack_rows(rows).astype(BF16)


def attend(slots, lengths, gathered, stats, full_t, grad_t, head_width):
    groups, slabs, packed_rows, lanes = gathered.shape
    resp_count, channels, columns = full_t.shape
    key_span = slabs * packed_rows * lanes // channels
    latent_width = grad_t.shape[1]
    grid_spec = pltpu.PrefetchScalarGridSpec(
        num_scalar_prefetch=2,
        grid=(resp_count,),
        in_specs=[
            pl.BlockSpec((1, slabs, packed_rows, lanes), lambda j, s, n: (s[j], 0, 0, 0)),
            pl.BlockSpec((1, 8, columns), lambda j, s, n: (j, 0, 0)),
            pl.BlockSpec((1, channels, columns), lambda j, s, n: (j, 0, 0)),
            pl.BlockSpec((1, latent_width, columns), lambda j, s, n: (j, 0, 0)),
        ],
        out_specs=[
            pl.BlockSpec((1, key_span, columns), lambda j, s, n: (j, 0, 0)),
            pl.BlockSpec((1, 8, columns), lambda j, s, n: (j, 0, 0)),
            pl.BlockSpec((groups, slabs, packed_rows, lanes), lambda j, s, n: (0, 0, 0, 0)),
        ],
        scratch_shapes=[
            pltpu.VMEM((groups, key_span, channels), F32),
            pltpu.VMEM((key_span, columns), BF16),
        ],
    )
    return pl.pallas_call(
        functools.partial(attend_kernel, head_width),
        grid_spec=grid_spec,
        out_shape=[
            jax.ShapeDtypeStruct((resp_count, key_span, columns), BF16),
            jax.ShapeDtypeStruct((resp_count, 8, columns), F32),
            jax.ShapeDtypeStruct((groups, slabs, packed_rows, lanes), BF16),
        ],
        compiler_params=pltpu.CompilerParams(vmem_limit_bytes=20*1024*1024),
        cost_estimate=pl.CostEstimate(
            flops=2 * resp_count * columns * key_span * 2176,
            bytes_accessed=30 * 1024 * 1024,
            transcendentals=resp_count * columns * key_span,
        ),
        name="attend",
    )(slots, lengths, gathered, stats, full_t, grad_t)


def output_kernel(slot_ref, latent_ref, own_ref, aT_ref, e_ref, ratio_ref, uv_ref, out_ref):
    rows = own_ref.shape[0]
    heads, latent_width, value_width = uv_ref.shape
    slab = aT_ref.shape[1] // latent_ref.shape[1]
    values = jnp.concatenate(
        [unpack_latent(latent_ref, slab), own_ref[:, pl.ds(0, latent_width)]], axis=0
    )
    values_t = values.T
    for i in range(0, heads, 2):
        at = pl.ds(i * rows, 2 * rows)
        own = (e_ref[0, :, at].astype(F32) * ratio_ref[0, pl.ds(0, 1), at]).astype(BF16)
        weights = jnp.concatenate([aT_ref[0, :, at], own], axis=0)
        latent_t = dot_nn(values_t, weights).astype(BF16)
        for e in range(2):
            part = latent_t[:, e * rows : (e + 1) * rows].T
            done = dot_nn(part, uv_ref[i + e])
            out_ref[:, pl.ds((i + e) * value_width, value_width)] = done.astype(BF16)


def outputs(slots, gathered, resp_latent, attention_t, own_weights, ratio, up_value):
    groups, slabs, packed_rows, lanes = gathered.shape
    resp_count, key_span, columns = attention_t.shape
    channels = resp_latent.shape[1]
    heads, latent_width, value_width = up_value.shape
    rows = resp_latent.shape[0] // resp_count
    grid_spec = pltpu.PrefetchScalarGridSpec(
        num_scalar_prefetch=1,
        grid=(resp_count,),
        in_specs=[
            pl.BlockSpec((1, slabs, packed_rows, lanes), lambda j, s: (s[j], 0, 0, 0)),
            pl.BlockSpec((rows, channels), lambda j, s: (j, 0)),
            pl.BlockSpec((1, key_span, columns), lambda j, s: (j, 0, 0)),
            pl.BlockSpec((1, rows, columns), lambda j, s: (j, 0, 0)),
            pl.BlockSpec((1, 8, columns), lambda j, s: (j, 0, 0)),
            pl.BlockSpec((heads, latent_width, value_width), lambda j, s: (0, 0, 0)),
        ],
        out_specs=pl.BlockSpec((rows, heads * value_width), lambda j, s: (j, 0)),
    )
    return pl.pallas_call(
        output_kernel,
        grid_spec=grid_spec,
        out_shape=jax.ShapeDtypeStruct((resp_count * rows, heads * value_width), BF16),
        compiler_params=pltpu.CompilerParams(vmem_limit_bytes=12*1024*1024),
        cost_estimate=pl.CostEstimate(
            flops=2 * resp_count * columns * (384 + 128) * 512,
            bytes_accessed=16 * 1024 * 1024,
            transcendentals=0,
        ),
        name="outputs",
    )(slots, gathered, resp_latent, attention_t, own_weights, ratio, up_value)


def on_device(
    queries, up_key, up_value, prompt_latent, resp_latent, grad_out, response_prompt, prompt_length
):
    groups = lax.axis_size("resp")
    slab_count = lax.axis_size("head")
    my_group = lax.axis_index("resp")
    owned, slab_rows, channels = prompt_latent.shape
    resp_count = response_prompt.shape[0] // groups
    owners = response_prompt // owned
    hit_table = owners[:, None] == jnp.arange(groups)[None, :]
    wanted = jnp.max(
        jnp.where(hit_table, (response_prompt % owned)[:, None], -1).reshape(
            groups, resp_count, groups
        ),
        axis=1,
    )
    wanted_mine = lax.dynamic_index_in_dim(wanted, my_group, 1, False)
    copies = pack(
        response_prompt, jnp.reshape(my_group, (1,)), prompt_latent, groups, slab_count
    ).reshape(groups * slab_count, -1, 128)
    arrived = lax.all_to_all(copies, ("resp", "head"), split_axis=0, concat_axis=0, tiled=True)
    gathered = arrived.reshape(groups, slab_count, -1, 128)
    local_prompt = lax.dynamic_slice_in_dim(response_prompt, my_group * resp_count, resp_count)
    slots = local_prompt // owned
    hits = local_prompt[:, None] == jnp.arange(prompt_length.shape[0])[None, :]
    lengths = jnp.sum(jnp.where(hits, prompt_length[None, :], 0), axis=1)
    head_width = queries.shape[1] // up_key.shape[0]
    full_t, grad_t = lift_tokens(queries, up_key, grad_out, up_value, resp_count)
    own_weights, stats = own_scores(resp_latent, full_t, grad_t, head_width)
    attention_t, ratio, pieces = attend(
        slots, lengths, gathered, stats, full_t, grad_t, head_width
    )
    returned_grad = lax.all_to_all(
        pieces.reshape(groups * slab_count, -1, 128),
        ("resp", "head"),
        split_axis=0,
        concat_axis=0,
        tiled=True,
    )
    attn_out = outputs(slots, gathered, resp_latent, attention_t, own_weights, ratio, up_value)
    summed = jnp.sum(returned_grad.reshape(groups, slab_count, -1, 128).astype(F32), axis=1)
    packed = jnp.stack(
        [
            jnp.sum(jnp.where((wanted_mine == p)[:, None, None], summed, 0.0), axis=0)
            for p in range(owned)
        ]
    )
    blocks = channels // 128
    latent = packed[:, : slab_rows * blocks].reshape(owned, blocks, slab_rows, 128)
    tail = packed[:, slab_rows * blocks :].reshape(owned, slab_rows // 2, 2, 64)
    prompt_grad = jnp.concatenate(
        [
            jnp.transpose(latent, (0, 2, 1, 3)).reshape(owned, slab_rows, blocks * 128),
            jnp.transpose(tail, (0, 2, 1, 3)).reshape(owned, slab_rows, 64),
        ],
        axis=2,
    )
    return (attn_out, prompt_grad)


def solution(mesh):
    return jax.shard_map(
        on_device,
        mesh=mesh,
        in_specs=(
            P("resp", "head"),
            P("head", None, None),
            P("head", None, None),
            P("resp", "head", None),
            P("resp", None),
            P("resp", "head"),
            P(),
            P(),
        ),
        out_specs=(P("resp", "head"), P("resp", "head", None)),
        check_vma=False,
    )
```

```python
import functools
import math

import jax
import jax.numpy as jnp
from jax import lax
from jax.experimental import pallas as pl
from jax.experimental.pallas import tpu as pltpu
from jax.sharding import PartitionSpec as P

BF16 = jnp.bfloat16
F32 = jnp.float32
LOG2E = 1.4426950408889634


def in_hbm(*arrays):
    return [pltpu.with_memory_space_constraint(a, pltpu.HBM) for a in arrays]


def dot_nn(a, b):
    return lax.dot_general(a, b, (((1,), (0,)), ((), ())), preferred_element_type=F32)


def dot_nt(a, b):
    return lax.dot_general(a, b, (((1,), (1,)), ((), ())), preferred_element_type=F32)


def up_kernel(q_ref, uk_ref, go_ref, uv_ref, fq_ref, gl_ref):
    resp_count, channels, _ = fq_ref.shape
    latent_width = gl_ref.shape[1]
    rope = channels - latent_width
    rows = q_ref.shape[0] // resp_count
    nope = uk_ref.shape[1]
    span = 2 * nope
    for e in range(2):
        lead = e * rope
        lift = uk_ref[e]
        parts = [lift, jnp.zeros((nope - lead, latent_width), BF16)]
        if lead:
            parts = [jnp.zeros((lead, latent_width), BF16)] + parts
        lifted = jnp.concatenate(parts, axis=0).T
        row = lax.broadcasted_iota(jnp.int32, (rope, span), 0)
        col = lax.broadcasted_iota(jnp.int32, (rope, span), 1)
        pick = jnp.where(col == row + (nope + lead), 1.0, 0.0).astype(BF16)
        up_value = uv_ref[e]
        for j in range(0, resp_count, 2):
            window = q_ref[pl.ds(j * rows, 2 * rows), pl.ds(e * nope, span)]
            grad = go_ref[pl.ds(j * rows, 2 * rows), pl.ds(e * rows, rows)]
            top = dot_nt(lifted, window).astype(BF16)
            low = dot_nt(pick, window).astype(BF16)
            lat = dot_nt(up_value, grad).astype(BF16)
            for i in range(2):
                src = slice(i * rows, (i + 1) * rows)
                dst = pl.ds(e * rows, rows)
                fq_ref[j + i, pl.ds(0, latent_width), dst] = top[:, src]
                fq_ref[j + i, pl.ds(latent_width, rope), dst] = low[:, src]
                gl_ref[j + i, :, dst] = lat[:, src]


def lift_tokens(queries, up_key, grad_out, up_value, resp_count):
    tokens = queries.shape[0]
    rows = tokens // resp_count
    heads, nope, latent_width = up_key.shape
    value_width = up_value.shape[2]
    head_width = queries.shape[1] // heads
    channels = latent_width + head_width - nope
    return pl.pallas_call(
        up_kernel,
        grid=(heads // 2,),
        in_specs=[
            pl.BlockSpec((tokens, 2 * head_width), lambda i: (0, i)),
            pl.BlockSpec((2, nope, latent_width), lambda i: (i, 0, 0)),
            pl.BlockSpec((tokens, 2 * value_width), lambda i: (0, i)),
            pl.BlockSpec((2, latent_width, value_width), lambda i: (i, 0, 0)),
        ],
        out_specs=[
            pl.BlockSpec((resp_count, channels, 2 * rows), lambda i: (0, 0, i)),
            pl.BlockSpec((resp_count, latent_width, 2 * rows), lambda i: (0, 0, i)),
        ],
        out_shape=[
            pltpu.HBM((resp_count, channels, heads * rows), BF16),
            pltpu.HBM((resp_count, latent_width, heads * rows), BF16),
        ],
        compiler_params=pltpu.CompilerParams(vmem_limit_bytes=14*1024*1024),
        cost_estimate=pl.CostEstimate(
            flops=4 * tokens * heads * nope * latent_width,
            bytes_accessed=30 * 1024 * 1024,
            transcendentals=0,
        ),
        name="lift_tokens",
    )(*in_hbm(queries, up_key, grad_out, up_value))


def pack_rows(rows):
    slab, channels = rows.shape
    blocks = channels // 128
    half = slab // 2
    tail = jnp.concatenate([rows[:half, 128 * blocks :], rows[half:, 128 * blocks :]], axis=1)
    return jnp.concatenate([rows[:, 128 * c : 128 * (c + 1)] for c in range(blocks)] + [tail], axis=0)


def pack_kernel(prompt_ref, group_ref, latent_ref, out_ref):
    groups, slab_count, packed_rows, lanes = out_ref.shape
    owned = latent_ref.shape[0]
    resp_count = prompt_ref.shape[0] // groups
    packed = [pack_rows(latent_ref[p].astype(F32)) for p in range(owned)]
    for r in range(groups):
        wanted = jnp.int32(-1)
        for i in range(resp_count):
            prompt = prompt_ref[r * resp_count + i]
            wanted = jnp.where(prompt // owned == group_ref[0], prompt % owned, wanted)
        chosen = packed[0]
        for p in range(1, owned):
            chosen = jnp.where(wanted == p, packed[p], chosen)
        chosen = chosen.astype(BF16)
        out_ref[r] = jnp.broadcast_to(chosen[None], (slab_count, packed_rows, lanes))


def pack(response_prompt, my_group, prompt_latent, groups, slab_count):
    owned, slab_rows, channels = prompt_latent.shape
    packed_rows = slab_rows * channels // 128
    return pl.pallas_call(
        pack_kernel,
        grid_spec=pltpu.PrefetchScalarGridSpec(
            num_scalar_prefetch=2,
            grid=(1,),
            in_specs=[pl.BlockSpec((owned, slab_rows, channels), lambda i, p, g: (0, 0, 0))],
            out_specs=pl.BlockSpec(
                (groups, slab_count, packed_rows, 128), lambda i, p, g: (0, 0, 0, 0)
            ),
        ),
        out_shape=jax.ShapeDtypeStruct((groups, slab_count, packed_rows, 128), BF16),
        compiler_params=pltpu.CompilerParams(vmem_limit_bytes=10 * 1024 * 1024),
        name="pack",
    )(response_prompt, my_group, *in_hbm(prompt_latent))


def own_kernel(head_width, own_ref, fq_ref, gl_ref, e_ref, stat_ref):
    rows = own_ref.shape[0]
    latent_width = gl_ref.shape[1]
    columns = fq_ref.shape[2]
    scaling = LOG2E / math.sqrt(head_width)
    chunk = 2 * rows
    keys = own_ref[...]
    values = keys[:, :latent_width]
    row = lax.broadcasted_iota(jnp.int32, (rows, chunk), 0)
    col = lax.broadcasted_iota(jnp.int32, (rows, chunk), 1) % rows
    allowed = row <= col
    for c in range(columns // chunk):
        at = pl.ds(c * chunk, chunk)
        scores = dot_nn(keys, fq_ref[0, :, at])
        grad_att = dot_nn(values, gl_ref[0, :, at])
        scores = jnp.where(allowed, scores * scaling, -1e30)
        top = jnp.max(scores, axis=0, keepdims=True)
        weights = jnp.exp2(scores - top)
        e_ref[0, :, at] = weights.astype(BF16)
        stat_ref[0, pl.ds(0, 1), at] = top
        stat_ref[0, pl.ds(1, 1), at] = jnp.sum(weights, axis=0, keepdims=True)
        stat_ref[0, pl.ds(2, 1), at] = jnp.sum(weights * grad_att, axis=0, keepdims=True)


def own_scores(resp_latent, full_t, grad_t, head_width):
    resp_count, channels, columns = full_t.shape
    latent_width = grad_t.shape[1]
    rows = resp_latent.shape[0] // resp_count
    return pl.pallas_call(
        functools.partial(own_kernel, head_width),
        grid=(resp_count,),
        in_specs=[
            pl.BlockSpec((rows, channels), lambda j: (j, 0)),
            pl.BlockSpec((1, channels, columns), lambda j: (j, 0, 0)),
            pl.BlockSpec((1, latent_width, columns), lambda j: (j, 0, 0)),
        ],
        out_specs=[
            pl.BlockSpec((1, rows, columns), lambda j: (j, 0, 0)),
            pl.BlockSpec((1, 8, columns), lambda j: (j, 0, 0)),
        ],
        out_shape=[
            pltpu.HBM((resp_count, rows, columns), BF16),
            pltpu.HBM((resp_count, 8, columns), F32),
        ],
        compiler_params=pltpu.CompilerParams(vmem_limit_bytes=10*1024*1024),
        cost_estimate=pl.CostEstimate(
            flops=2 * resp_count * columns * rows * (channels + latent_width),
            bytes_accessed=22 * 1024 * 1024,
            transcendentals=resp_count * columns * rows,
        ),
        name="own_scores",
    )(*in_hbm(resp_latent, full_t, grad_t))


def unpack_latent(packed_ref, slab):
    slabs, packed_rows, lanes = packed_ref.shape[1:]
    return jnp.concatenate(
        [
            jnp.concatenate(
                [packed_ref[0, h, pl.ds(slab * c, slab), :] for h in range(slabs)], axis=0
            )
            for c in range(packed_rows // slab)
        ],
        axis=1,
    )


def unpack_rope(packed_ref, slab):
    slabs, packed_rows, lanes = packed_ref.shape[1:]
    rows = []
    for h in range(slabs):
        tail = packed_ref[0, h].astype(F32)[packed_rows - slab // 2 :]
        rows += [tail[:, : lanes // 2], tail[:, lanes // 2 :]]
    return jnp.concatenate(rows, axis=0).astype(BF16)


def attend_kernel(
    head_width,
    slot_ref,
    len_ref,
    latent_ref,
    stat_ref,
    fq_ref,
    gl_ref,
    aT_ref,
    ratio_ref,
    piece_ref,
    acc_ref,
    gs_ref,
):
    j = pl.program_id(0)
    steps = pl.num_programs(0)
    channels = fq_ref.shape[1]
    latent_width = gl_ref.shape[1]
    columns = fq_ref.shape[2]
    rope = channels - latent_width
    groups, key_span, _ = acc_ref.shape
    slabs = latent_ref.shape[1]
    slab = key_span // slabs
    scaling = 1.0 / math.sqrt(head_width)
    chunk = 256

    @pl.when(j == 0)
    def _():
        acc_ref[...] = jnp.zeros_like(acc_ref)

    length = len_ref[j]
    values = unpack_latent(latent_ref, slab)
    keys = jnp.concatenate([values, unpack_rope(latent_ref, slab)], axis=1)
    row = lax.broadcasted_iota(jnp.int32, (key_span, chunk), 0)
    allowed = row < length
    for c in range(columns // chunk):
        at = pl.ds(c * chunk, chunk)
        scores = dot_nn(keys, fq_ref[0, :, at])
        grad_att = dot_nn(values, gl_ref[0, :, at])
        own_top = stat_ref[0, pl.ds(0, 1), at]
        scores = jnp.where(allowed, scores * (scaling * LOG2E), -1e30)
        top = jnp.maximum(jnp.max(scores, axis=0, keepdims=True), own_top)
        weights = jnp.exp2(scores - top)
        shift = jnp.exp2(own_top - top)
        total = jnp.sum(weights, axis=0, keepdims=True) + shift * stat_ref[0, pl.ds(1, 1), at]
        inverse = 1.0 / total
        inner = jnp.sum(weights * grad_att, axis=0, keepdims=True)
        inner = (inner + shift * stat_ref[0, pl.ds(2, 1), at]) * inverse
        attention = weights * inverse
        aT_ref[0, :, at] = attention.astype(BF16)
        gs_ref[:, at] = (attention * ((grad_att - inner) * scaling)).astype(BF16)
        ratio_ref[0, pl.ds(0, 1), at] = shift * inverse
    combined = dot_nt(gs_ref[...], fq_ref[0])
    value_term = dot_nt(aT_ref[0], gl_ref[0])
    slot = slot_ref[j]
    acc_ref[slot, :, pl.ds(0, latent_width)] += combined[:, :latent_width] + value_term
    acc_ref[slot, :, pl.ds(latent_width, rope)] += combined[:, latent_width:]

    @pl.when(j == steps - 1)
    def _():
        for g in range(groups):
            for h in range(slabs):
                rows = acc_ref[g, pl.ds(h * slab, slab), :]
                piece_ref[g, h] = pack_rows(rows).astype(BF16)


def attend(slots, lengths, gathered, stats, full_t, grad_t, head_width):
    groups, slabs, packed_rows, lanes = gathered.shape
    resp_count, channels, columns = full_t.shape
    key_span = slabs * packed_rows * lanes // channels
    latent_width = grad_t.shape[1]
    grid_spec = pltpu.PrefetchScalarGridSpec(
        num_scalar_prefetch=2,
        grid=(resp_count,),
        in_specs=[
            pl.BlockSpec((1, slabs, packed_rows, lanes), lambda j, s, n: (s[j], 0, 0, 0)),
            pl.BlockSpec((1, 8, columns), lambda j, s, n: (j, 0, 0)),
            pl.BlockSpec((1, channels, columns), lambda j, s, n: (j, 0, 0)),
            pl.BlockSpec((1, latent_width, columns), lambda j, s, n: (j, 0, 0)),
        ],
        out_specs=[
            pl.BlockSpec((1, key_span, columns), lambda j, s, n: (j, 0, 0)),
            pl.BlockSpec((1, 8, columns), lambda j, s, n: (j, 0, 0)),
            pl.BlockSpec((groups, slabs, packed_rows, lanes), lambda j, s, n: (0, 0, 0, 0)),
        ],
        scratch_shapes=[
            pltpu.VMEM((groups, key_span, channels), F32),
            pltpu.VMEM((key_span, columns), BF16),
        ],
    )
    return pl.pallas_call(
        functools.partial(attend_kernel, head_width),
        grid_spec=grid_spec,
        out_shape=[
            pltpu.HBM((resp_count, key_span, columns), BF16),
            pltpu.HBM((resp_count, 8, columns), F32),
            pltpu.HBM((groups, slabs, packed_rows, lanes), BF16),
        ],
        compiler_params=pltpu.CompilerParams(vmem_limit_bytes=20*1024*1024),
        cost_estimate=pl.CostEstimate(
            flops=2 * resp_count * columns * key_span * 2176,
            bytes_accessed=30 * 1024 * 1024,
            transcendentals=resp_count * columns * key_span,
        ),
        name="attend",
    )(slots, lengths, *in_hbm(gathered, stats, full_t, grad_t))


def output_kernel(slot_ref, latent_ref, own_ref, aT_ref, e_ref, ratio_ref, uv_ref, out_ref):
    rows = own_ref.shape[0]
    heads, latent_width, value_width = uv_ref.shape
    slab = aT_ref.shape[1] // latent_ref.shape[1]
    values = jnp.concatenate(
        [unpack_latent(latent_ref, slab), own_ref[:, pl.ds(0, latent_width)]], axis=0
    )
    values_t = values.T
    for i in range(0, heads, 2):
        at = pl.ds(i * rows, 2 * rows)
        own = (e_ref[0, :, at].astype(F32) * ratio_ref[0, pl.ds(0, 1), at]).astype(BF16)
        weights = jnp.concatenate([aT_ref[0, :, at], own], axis=0)
        latent_t = dot_nn(values_t, weights).astype(BF16)
        for e in range(2):
            part = latent_t[:, e * rows : (e + 1) * rows].T
            done = dot_nn(part, uv_ref[i + e])
            out_ref[:, pl.ds((i + e) * value_width, value_width)] = done.astype(BF16)


def outputs(slots, gathered, resp_latent, attention_t, own_weights, ratio, up_value):
    groups, slabs, packed_rows, lanes = gathered.shape
    resp_count, key_span, columns = attention_t.shape
    channels = resp_latent.shape[1]
    heads, latent_width, value_width = up_value.shape
    rows = resp_latent.shape[0] // resp_count
    grid_spec = pltpu.PrefetchScalarGridSpec(
        num_scalar_prefetch=1,
        grid=(resp_count,),
        in_specs=[
            pl.BlockSpec((1, slabs, packed_rows, lanes), lambda j, s: (s[j], 0, 0, 0)),
            pl.BlockSpec((rows, channels), lambda j, s: (j, 0)),
            pl.BlockSpec((1, key_span, columns), lambda j, s: (j, 0, 0)),
            pl.BlockSpec((1, rows, columns), lambda j, s: (j, 0, 0)),
            pl.BlockSpec((1, 8, columns), lambda j, s: (j, 0, 0)),
            pl.BlockSpec((heads, latent_width, value_width), lambda j, s: (0, 0, 0)),
        ],
        out_specs=pl.BlockSpec((rows, heads * value_width), lambda j, s: (j, 0)),
    )
    return pl.pallas_call(
        output_kernel,
        grid_spec=grid_spec,
        out_shape=jax.ShapeDtypeStruct((resp_count * rows, heads * value_width), BF16),
        compiler_params=pltpu.CompilerParams(vmem_limit_bytes=12*1024*1024),
        cost_estimate=pl.CostEstimate(
            flops=2 * resp_count * columns * (384 + 128) * 512,
            bytes_accessed=16 * 1024 * 1024,
            transcendentals=0,
        ),
        name="outputs",
    )(
        slots,
        *in_hbm(gathered, resp_latent, attention_t, own_weights, ratio, up_value),
    )


def on_device(
    queries, up_key, up_value, prompt_latent, resp_latent, grad_out, response_prompt, prompt_length
):
    groups = lax.axis_size("resp")
    slab_count = lax.axis_size("head")
    my_group = lax.axis_index("resp")
    owned, slab_rows, channels = prompt_latent.shape
    resp_count = response_prompt.shape[0] // groups
    owners = response_prompt // owned
    hit_table = owners[:, None] == jnp.arange(groups)[None, :]
    wanted = jnp.max(
        jnp.where(hit_table, (response_prompt % owned)[:, None], -1).reshape(
            groups, resp_count, groups
        ),
        axis=1,
    )
    wanted_mine = lax.dynamic_index_in_dim(wanted, my_group, 1, False)
    copies = pack(
        response_prompt, jnp.reshape(my_group, (1,)), prompt_latent, groups, slab_count
    ).reshape(groups * slab_count, -1, 128)
    arrived = lax.all_to_all(copies, ("resp", "head"), split_axis=0, concat_axis=0, tiled=True)
    gathered = arrived.reshape(groups, slab_count, -1, 128)
    local_prompt = lax.dynamic_slice_in_dim(response_prompt, my_group * resp_count, resp_count)
    slots = local_prompt // owned
    hits = local_prompt[:, None] == jnp.arange(prompt_length.shape[0])[None, :]
    lengths = jnp.sum(jnp.where(hits, prompt_length[None, :], 0), axis=1)
    head_width = queries.shape[1] // up_key.shape[0]
    full_t, grad_t = lift_tokens(queries, up_key, grad_out, up_value, resp_count)
    own_weights, stats = own_scores(resp_latent, full_t, grad_t, head_width)
    attention_t, ratio, pieces = attend(
        slots, lengths, gathered, stats, full_t, grad_t, head_width
    )
    returned_grad = lax.all_to_all(
        pieces.reshape(groups * slab_count, -1, 128),
        ("resp", "head"),
        split_axis=0,
        concat_axis=0,
        tiled=True,
    )
    attn_out = outputs(slots, gathered, resp_latent, attention_t, own_weights, ratio, up_value)
    summed = jnp.sum(returned_grad.reshape(groups, slab_count, -1, 128).astype(F32), axis=1)
    packed = jnp.stack(
        [
            jnp.sum(jnp.where((wanted_mine == p)[:, None, None], summed, 0.0), axis=0)
            for p in range(owned)
        ]
    )
    blocks = channels // 128
    latent = packed[:, : slab_rows * blocks].reshape(owned, blocks, slab_rows, 128)
    tail = packed[:, slab_rows * blocks :].reshape(owned, slab_rows // 2, 2, 64)
    prompt_grad = jnp.concatenate(
        [
            jnp.transpose(latent, (0, 2, 1, 3)).reshape(owned, slab_rows, blocks * 128),
            jnp.transpose(tail, (0, 2, 1, 3)).reshape(owned, slab_rows, 64),
        ],
        axis=2,
    )
    return (attn_out, prompt_grad)


def solution(mesh):
    return jax.shard_map(
        on_device,
        mesh=mesh,
        in_specs=(
            P("resp", "head"),
            P("head", None, None),
            P("head", None, None),
            P("resp", "head", None),
            P("resp", None),
            P("resp", "head"),
            P(),
            P(),
        ),
        out_specs=(P("resp", "head"), P("resp", "head", None)),
        check_vma=False,
    )
```

```python
import functools
import math

import jax
import jax.numpy as jnp
from jax import lax
from jax.experimental import pallas as pl
from jax.experimental.pallas import tpu as pltpu
from jax.sharding import PartitionSpec as P

BF16 = jnp.bfloat16
F32 = jnp.float32
LOG2E = 1.4426950408889634


def in_hbm(*arrays):
    return [pltpu.with_memory_space_constraint(a, pltpu.HBM) for a in arrays]


def dot_nn(a, b):
    return lax.dot_general(a, b, (((1,), (0,)), ((), ())), preferred_element_type=F32)


def dot_nt(a, b):
    return lax.dot_general(a, b, (((1,), (1,)), ((), ())), preferred_element_type=F32)


def up_kernel(q_ref, uk_ref, go_ref, uv_ref, fq_ref, gl_ref):
    resp_count, channels, _ = fq_ref.shape
    latent_width = gl_ref.shape[1]
    rope = channels - latent_width
    rows = q_ref.shape[0] // resp_count
    nope = uk_ref.shape[1]
    span = 2 * nope
    for e in range(2):
        lead = e * rope
        lift = uk_ref[e]
        parts = [lift, jnp.zeros((nope - lead, latent_width), BF16)]
        if lead:
            parts = [jnp.zeros((lead, latent_width), BF16)] + parts
        lifted = jnp.concatenate(parts, axis=0).T
        row = lax.broadcasted_iota(jnp.int32, (rope, span), 0)
        col = lax.broadcasted_iota(jnp.int32, (rope, span), 1)
        pick = jnp.where(col == row + (nope + lead), 1.0, 0.0).astype(BF16)
        up_value = uv_ref[e]
        for j in range(0, resp_count, 2):
            window = q_ref[pl.ds(j * rows, 2 * rows), pl.ds(e * nope, span)]
            grad = go_ref[pl.ds(j * rows, 2 * rows), pl.ds(e * rows, rows)]
            top = dot_nt(lifted, window).astype(BF16)
            low = dot_nt(pick, window).astype(BF16)
            lat = dot_nt(up_value, grad).astype(BF16)
            for i in range(2):
                src = slice(i * rows, (i + 1) * rows)
                dst = pl.ds(e * rows, rows)
                fq_ref[j + i, pl.ds(0, latent_width), dst] = top[:, src]
                fq_ref[j + i, pl.ds(latent_width, rope), dst] = low[:, src]
                gl_ref[j + i, :, dst] = lat[:, src]


def lift_tokens(queries, up_key, grad_out, up_value, resp_count):
    tokens = queries.shape[0]
    rows = tokens // resp_count
    heads, nope, latent_width = up_key.shape
    value_width = up_value.shape[2]
    head_width = queries.shape[1] // heads
    channels = latent_width + head_width - nope
    return pl.pallas_call(
        up_kernel,
        grid=(heads // 2,),
        in_specs=[
            pl.BlockSpec((tokens, 2 * head_width), lambda i: (0, i)),
            pl.BlockSpec((2, nope, latent_width), lambda i: (i, 0, 0)),
            pl.BlockSpec((tokens, 2 * value_width), lambda i: (0, i)),
            pl.BlockSpec((2, latent_width, value_width), lambda i: (i, 0, 0)),
        ],
        out_specs=[
            pl.BlockSpec((resp_count, channels, 2 * rows), lambda i: (0, 0, i)),
            pl.BlockSpec((resp_count, latent_width, 2 * rows), lambda i: (0, 0, i)),
        ],
        out_shape=[
            pltpu.HBM((resp_count, channels, heads * rows), BF16),
            pltpu.HBM((resp_count, latent_width, heads * rows), BF16),
        ],
        compiler_params=pltpu.CompilerParams(vmem_limit_bytes=14*1024*1024),
        cost_estimate=pl.CostEstimate(
            flops=4 * tokens * heads * nope * latent_width,
            bytes_accessed=30 * 1024 * 1024,
            transcendentals=0,
        ),
        name="lift_tokens",
    )(*in_hbm(queries, up_key, grad_out, up_value))


def pack_rows(rows):
    slab, channels = rows.shape
    blocks = channels // 128
    half = slab // 2
    tail = jnp.concatenate([rows[:half, 128 * blocks :], rows[half:, 128 * blocks :]], axis=1)
    return jnp.concatenate([rows[:, 128 * c : 128 * (c + 1)] for c in range(blocks)] + [tail], axis=0)


def pack_kernel(axis, prompt_any, latent_any, out_ref, prompt_ref, latent_ref, sem):
    copies = [
        pltpu.make_async_copy(prompt_any, prompt_ref, sem.at[0]),
        pltpu.make_async_copy(latent_any, latent_ref, sem.at[1]),
    ]
    for copy in copies:
        copy.start()
    for copy in copies:
        copy.wait()
    groups, slab_count, packed_rows, lanes = out_ref.shape
    owned = latent_ref.shape[0]
    resp_count = prompt_ref.shape[0] // groups
    first = lax.axis_index(axis) * owned
    packed = [pack_rows(latent_ref[p].astype(F32)).astype(BF16) for p in range(owned)]
    for r in range(groups):
        chosen = packed[0]
        for p in range(1, owned):
            hits = [prompt_ref[r * resp_count + i] == first + p for i in range(resp_count)]
            chosen = jnp.where(functools.reduce(jnp.logical_or, hits), packed[p], chosen)
        out_ref[r] = jnp.broadcast_to(chosen[None], (slab_count, packed_rows, lanes))


def pack(response_prompt, prompt_latent, groups, slab_count):
    owned, slab_rows, channels = prompt_latent.shape
    packed_rows = slab_rows * channels // 128
    return pl.pallas_call(
        functools.partial(pack_kernel, "resp"),
        in_specs=[pl.BlockSpec(memory_space=pl.ANY)] * 2,
        out_specs=pl.BlockSpec(memory_space=pltpu.VMEM),
        scratch_shapes=[
            pltpu.SMEM(response_prompt.shape, response_prompt.dtype),
            pltpu.VMEM(prompt_latent.shape, BF16),
            pltpu.SemaphoreType.DMA((2,)),
        ],
        out_shape=pltpu.VMEM((groups, slab_count, packed_rows, 128), BF16),
        compiler_params=pltpu.CompilerParams(vmem_limit_bytes=10 * 1024 * 1024),
        name="pack",
    )(*in_hbm(response_prompt, prompt_latent))


def own_kernel(head_width, own_ref, fq_ref, gl_ref, e_ref, stat_ref):
    rows = own_ref.shape[0]
    latent_width = gl_ref.shape[1]
    columns = fq_ref.shape[2]
    scaling = LOG2E / math.sqrt(head_width)
    chunk = 2 * rows
    keys = own_ref[...]
    values = keys[:, :latent_width]
    row = lax.broadcasted_iota(jnp.int32, (rows, chunk), 0)
    col = lax.broadcasted_iota(jnp.int32, (rows, chunk), 1) % rows
    allowed = row <= col
    for c in range(columns // chunk):
        at = pl.ds(c * chunk, chunk)
        scores = dot_nn(keys, fq_ref[0, :, at])
        grad_att = dot_nn(values, gl_ref[0, :, at])
        scores = jnp.where(allowed, scores * scaling, -1e30)
        top = jnp.max(scores, axis=0, keepdims=True)
        weights = jnp.exp2(scores - top)
        e_ref[0, :, at] = weights.astype(BF16)
        stat_ref[0, pl.ds(0, 1), at] = top
        stat_ref[0, pl.ds(1, 1), at] = jnp.sum(weights, axis=0, keepdims=True)
        stat_ref[0, pl.ds(2, 1), at] = jnp.sum(weights * grad_att, axis=0, keepdims=True)


def own_scores(resp_latent, full_t, grad_t, head_width):
    resp_count, channels, columns = full_t.shape
    latent_width = grad_t.shape[1]
    rows = resp_latent.shape[0] // resp_count
    return pl.pallas_call(
        functools.partial(own_kernel, head_width),
        grid=(resp_count,),
        in_specs=[
            pl.BlockSpec((rows, channels), lambda j: (j, 0)),
            pl.BlockSpec((1, channels, columns), lambda j: (j, 0, 0)),
            pl.BlockSpec((1, latent_width, columns), lambda j: (j, 0, 0)),
        ],
        out_specs=[
            pl.BlockSpec((1, rows, columns), lambda j: (j, 0, 0)),
            pl.BlockSpec((1, 8, columns), lambda j: (j, 0, 0)),
        ],
        out_shape=[
            pltpu.HBM((resp_count, rows, columns), BF16),
            pltpu.HBM((resp_count, 8, columns), F32),
        ],
        compiler_params=pltpu.CompilerParams(vmem_limit_bytes=10*1024*1024),
        cost_estimate=pl.CostEstimate(
            flops=2 * resp_count * columns * rows * (channels + latent_width),
            bytes_accessed=22 * 1024 * 1024,
            transcendentals=resp_count * columns * rows,
        ),
        name="own_scores",
    )(*in_hbm(resp_latent, full_t, grad_t))


def unpack_latent(packed_ref, slab):
    slabs, packed_rows, lanes = packed_ref.shape[1:]
    return jnp.concatenate(
        [
            jnp.concatenate(
                [packed_ref[0, h, pl.ds(slab * c, slab), :] for h in range(slabs)], axis=0
            )
            for c in range(packed_rows // slab)
        ],
        axis=1,
    )


def unpack_rope(packed_ref, slab):
    slabs, packed_rows, lanes = packed_ref.shape[1:]
    rows = []
    for h in range(slabs):
        tail = packed_ref[0, h].astype(F32)[packed_rows - slab // 2 :]
        rows += [tail[:, : lanes // 2], tail[:, lanes // 2 :]]
    return jnp.concatenate(rows, axis=0).astype(BF16)


def attend_kernel(
    head_width,
    slot_ref,
    len_ref,
    latent_ref,
    stat_ref,
    fq_ref,
    gl_ref,
    aT_ref,
    ratio_ref,
    value_ref,
    piece_ref,
    acc_ref,
    gs_ref,
):
    j = pl.program_id(0)
    channels = fq_ref.shape[1]
    latent_width = gl_ref.shape[1]
    columns = fq_ref.shape[2]
    rope = channels - latent_width
    groups, key_span, _ = acc_ref.shape
    slabs = latent_ref.shape[1]
    slab = key_span // slabs
    scaling = 1.0 / math.sqrt(head_width)
    chunk = 256

    slot = slot_ref[j]
    length = len_ref[j]
    seen = jnp.int32(0)
    for k in range(slot_ref.shape[0]):
        seen = jnp.where((k < j) & (slot_ref[k] == slot), 1, seen)
    values = unpack_latent(latent_ref, slab)
    value_ref[0] = values
    keys = jnp.concatenate([values, unpack_rope(latent_ref, slab)], axis=1)
    row = lax.broadcasted_iota(jnp.int32, (key_span, chunk), 0)
    allowed = row < length
    for c in range(columns // chunk):
        at = pl.ds(c * chunk, chunk)
        scores = dot_nn(keys, fq_ref[0, :, at])
        grad_att = dot_nn(values, gl_ref[0, :, at])
        own_top = stat_ref[0, pl.ds(0, 1), at]
        scores = jnp.where(allowed, scores * (scaling * LOG2E), -1e30)
        top = jnp.maximum(jnp.max(scores, axis=0, keepdims=True), own_top)
        weights = jnp.exp2(scores - top)
        shift = jnp.exp2(own_top - top)
        total = jnp.sum(weights, axis=0, keepdims=True) + shift * stat_ref[0, pl.ds(1, 1), at]
        inverse = 1.0 / total
        inner = jnp.sum(weights * grad_att, axis=0, keepdims=True)
        inner = (inner + shift * stat_ref[0, pl.ds(2, 1), at]) * inverse
        attention = weights * inverse
        aT_ref[0, :, at] = attention.astype(BF16)
        gs_ref[:, at] = (attention * ((grad_att - inner) * scaling)).astype(BF16)
        ratio_ref[0, pl.ds(0, 1), at] = shift * inverse
    combined = dot_nt(gs_ref[...], fq_ref[0])
    value_term = dot_nt(aT_ref[0], gl_ref[0])
    latent_part = combined[:, :latent_width] + value_term
    rope_part = combined[:, latent_width:]
    earlier = acc_ref[slot]
    latent_part += jnp.where(seen == 1, earlier[:, :latent_width], 0.0)
    rope_part += jnp.where(seen == 1, earlier[:, latent_width:], 0.0)
    acc_ref[slot, :, pl.ds(0, latent_width)] = latent_part
    acc_ref[slot, :, pl.ds(latent_width, rope)] = rope_part
    for h in range(slabs):
        piece_ref[0, h] = pack_rows(acc_ref[slot, pl.ds(h * slab, slab), :]).astype(BF16)


def attend(slots, lengths, gathered, stats, full_t, grad_t, head_width):
    groups, slabs, packed_rows, lanes = gathered.shape
    resp_count, channels, columns = full_t.shape
    key_span = slabs * packed_rows * lanes // channels
    latent_width = grad_t.shape[1]
    grid_spec = pltpu.PrefetchScalarGridSpec(
        num_scalar_prefetch=2,
        grid=(resp_count,),
        in_specs=[
            pl.BlockSpec((1, slabs, packed_rows, lanes), lambda j, s, n: (s[j], 0, 0, 0)),
            pl.BlockSpec((1, 8, columns), lambda j, s, n: (j, 0, 0)),
            pl.BlockSpec((1, channels, columns), lambda j, s, n: (j, 0, 0)),
            pl.BlockSpec((1, latent_width, columns), lambda j, s, n: (j, 0, 0)),
        ],
        out_specs=[
            pl.BlockSpec((1, key_span, columns), lambda j, s, n: (j, 0, 0)),
            pl.BlockSpec((1, 8, columns), lambda j, s, n: (j, 0, 0)),
            pl.BlockSpec((1, key_span, latent_width), lambda j, s, n: (j, 0, 0)),
            pl.BlockSpec((1, slabs, packed_rows, lanes), lambda j, s, n: (s[j], 0, 0, 0)),
        ],
        scratch_shapes=[
            pltpu.VMEM((groups, key_span, channels), F32),
            pltpu.VMEM((key_span, columns), BF16),
        ],
    )
    return pl.pallas_call(
        functools.partial(attend_kernel, head_width),
        grid_spec=grid_spec,
        out_shape=[
            pltpu.HBM((resp_count, key_span, columns), BF16),
            pltpu.HBM((resp_count, 8, columns), F32),
            pltpu.HBM((resp_count, key_span, latent_width), BF16),
            pltpu.HBM((groups, slabs, packed_rows, lanes), BF16),
        ],
        compiler_params=pltpu.CompilerParams(vmem_limit_bytes=20*1024*1024),
        cost_estimate=pl.CostEstimate(
            flops=2 * resp_count * columns * key_span * 2176,
            bytes_accessed=30 * 1024 * 1024,
            transcendentals=resp_count * columns * key_span,
        ),
        name="attend",
    )(slots, lengths, gathered, *in_hbm(stats, full_t, grad_t))


def output_kernel(latent_ref, own_ref, aT_ref, e_ref, ratio_ref, uv_ref, out_ref):
    rows = own_ref.shape[0]
    heads, latent_width, value_width = uv_ref.shape
    values = jnp.concatenate(
        [latent_ref[0], own_ref[:, pl.ds(0, latent_width)]], axis=0
    )
    values_t = values.T
    for i in range(0, heads, 2):
        at = pl.ds(i * rows, 2 * rows)
        own = (e_ref[0, :, at].astype(F32) * ratio_ref[0, pl.ds(0, 1), at]).astype(BF16)
        weights = jnp.concatenate([aT_ref[0, :, at], own], axis=0)
        latent_t = dot_nn(values_t, weights).astype(BF16)
        for e in range(2):
            part = latent_t[:, e * rows : (e + 1) * rows].T
            done = dot_nn(part, uv_ref[i + e])
            out_ref[:, pl.ds((i + e) * value_width, value_width)] = done.astype(BF16)


def outputs(prompt_values, resp_latent, attention_t, own_weights, ratio, up_value):
    resp_count, key_span, columns = attention_t.shape
    channels = resp_latent.shape[1]
    heads, latent_width, value_width = up_value.shape
    rows = resp_latent.shape[0] // resp_count
    return pl.pallas_call(
        output_kernel,
        grid=(resp_count,),
        in_specs=[
            pl.BlockSpec((1, key_span, latent_width), lambda j: (j, 0, 0)),
            pl.BlockSpec((rows, channels), lambda j: (j, 0)),
            pl.BlockSpec((1, key_span, columns), lambda j: (j, 0, 0)),
            pl.BlockSpec((1, rows, columns), lambda j: (j, 0, 0)),
            pl.BlockSpec((1, 8, columns), lambda j: (j, 0, 0)),
            pl.BlockSpec((heads, latent_width, value_width), lambda j: (0, 0, 0)),
        ],
        out_specs=pl.BlockSpec((rows, heads * value_width), lambda j: (j, 0)),
        out_shape=jax.ShapeDtypeStruct((resp_count * rows, heads * value_width), BF16),
        compiler_params=pltpu.CompilerParams(vmem_limit_bytes=12*1024*1024),
        cost_estimate=pl.CostEstimate(
            flops=2 * resp_count * columns * (384 + 128) * 512,
            bytes_accessed=16 * 1024 * 1024,
            transcendentals=0,
        ),
        name="outputs",
    )(*in_hbm(prompt_values, resp_latent, attention_t, own_weights, ratio, up_value))


def on_device(
    queries, up_key, up_value, prompt_latent, resp_latent, grad_out, response_prompt, prompt_length
):
    groups = lax.axis_size("resp")
    slab_count = lax.axis_size("head")
    my_group = lax.axis_index("resp")
    owned, slab_rows, channels = prompt_latent.shape
    resp_count = response_prompt.shape[0] // groups
    owners = response_prompt // owned
    hit_table = owners[:, None] == jnp.arange(groups)[None, :]
    wanted = jnp.max(
        jnp.where(hit_table, (response_prompt % owned)[:, None], -1).reshape(
            groups, resp_count, groups
        ),
        axis=1,
    )
    wanted_mine = lax.dynamic_index_in_dim(wanted, my_group, 1, False)
    copies = pack(response_prompt, prompt_latent, groups, slab_count)
    copies = copies.reshape(groups * slab_count, -1, 128)
    arrived = lax.all_to_all(copies, ("resp", "head"), split_axis=0, concat_axis=0, tiled=True)
    gathered = arrived.reshape(groups, slab_count, -1, 128)
    local_prompt = lax.dynamic_slice_in_dim(response_prompt, my_group * resp_count, resp_count)
    slots = local_prompt // owned
    hits = local_prompt[:, None] == jnp.arange(prompt_length.shape[0])[None, :]
    lengths = jnp.sum(jnp.where(hits, prompt_length[None, :], 0), axis=1)
    head_width = queries.shape[1] // up_key.shape[0]
    full_t, grad_t = lift_tokens(queries, up_key, grad_out, up_value, resp_count)
    own_weights, stats = own_scores(resp_latent, full_t, grad_t, head_width)
    attention_t, ratio, prompt_values, pieces = attend(
        slots, lengths, gathered, stats, full_t, grad_t, head_width
    )
    returned_grad = lax.all_to_all(
        pieces.reshape(groups * slab_count, -1, 128),
        ("resp", "head"),
        split_axis=0,
        concat_axis=0,
        tiled=True,
    )
    attn_out = outputs(prompt_values, resp_latent, attention_t, own_weights, ratio, up_value)
    summed = jnp.sum(returned_grad.reshape(groups, slab_count, -1, 128).astype(F32), axis=1)
    packed = jnp.stack(
        [
            jnp.sum(jnp.where((wanted_mine == p)[:, None, None], summed, 0.0), axis=0)
            for p in range(owned)
        ]
    )
    blocks = channels // 128
    latent = packed[:, : slab_rows * blocks].reshape(owned, blocks, slab_rows, 128)
    tail = packed[:, slab_rows * blocks :].reshape(owned, slab_rows // 2, 2, 64)
    prompt_grad = jnp.concatenate(
        [
            jnp.transpose(latent, (0, 2, 1, 3)).reshape(owned, slab_rows, blocks * 128),
            jnp.transpose(tail, (0, 2, 1, 3)).reshape(owned, slab_rows, 64),
        ],
        axis=2,
    )
    return (attn_out, prompt_grad)


def solution(mesh):
    return jax.shard_map(
        on_device,
        mesh=mesh,
        in_specs=(
            P("resp", "head"),
            P("head", None, None),
            P("head", None, None),
            P("resp", "head", None),
            P("resp", None),
            P("resp", "head"),
            P(),
            P(),
        ),
        out_specs=(P("resp", "head"), P("resp", "head", None)),
        check_vma=False,
    )
```

```python
import functools
import math

import jax
import jax.numpy as jnp
from jax import lax
from jax.experimental import pallas as pl
from jax.experimental.pallas import tpu as pltpu
from jax.sharding import PartitionSpec as P

BF16 = jnp.bfloat16
F32 = jnp.float32
LOG2E = 1.4426950408889634


def in_hbm(*arrays):
    return [pltpu.with_memory_space_constraint(a, pltpu.HBM) for a in arrays]


def dot_nn(a, b):
    return lax.dot_general(a, b, (((1,), (0,)), ((), ())), preferred_element_type=F32)


def dot_nt(a, b):
    return lax.dot_general(a, b, (((1,), (1,)), ((), ())), preferred_element_type=F32)


def up_kernel(q_ref, uk_ref, go_ref, uv_ref, fq_ref, gl_ref):
    resp_count, channels, _ = fq_ref.shape
    latent_width = gl_ref.shape[1]
    rope = channels - latent_width
    rows = q_ref.shape[0] // resp_count
    nope = uk_ref.shape[1]
    span = 2 * nope
    for e in range(2):
        lead = e * rope
        lift = uk_ref[e]
        parts = [lift, jnp.zeros((nope - lead, latent_width), BF16)]
        if lead:
            parts = [jnp.zeros((lead, latent_width), BF16)] + parts
        lifted = jnp.concatenate(parts, axis=0).T
        row = lax.broadcasted_iota(jnp.int32, (rope, span), 0)
        col = lax.broadcasted_iota(jnp.int32, (rope, span), 1)
        pick = jnp.where(col == row + (nope + lead), 1.0, 0.0).astype(BF16)
        up_value = uv_ref[e]
        for j in range(0, resp_count, 2):
            window = q_ref[pl.ds(j * rows, 2 * rows), pl.ds(e * nope, span)]
            grad = go_ref[pl.ds(j * rows, 2 * rows), pl.ds(e * rows, rows)]
            top = dot_nt(lifted, window).astype(BF16)
            low = dot_nt(pick, window).astype(BF16)
            lat = dot_nt(up_value, grad).astype(BF16)
            for i in range(2):
                src = slice(i * rows, (i + 1) * rows)
                dst = pl.ds(e * rows, rows)
                fq_ref[j + i, pl.ds(0, latent_width), dst] = top[:, src]
                fq_ref[j + i, pl.ds(latent_width, rope), dst] = low[:, src]
                gl_ref[j + i, :, dst] = lat[:, src]


def lift_tokens(queries, up_key, grad_out, up_value, resp_count):
    tokens = queries.shape[0]
    rows = tokens // resp_count
    heads, nope, latent_width = up_key.shape
    value_width = up_value.shape[2]
    head_width = queries.shape[1] // heads
    channels = latent_width + head_width - nope
    return pl.pallas_call(
        up_kernel,
        grid=(heads // 2,),
        in_specs=[
            pl.BlockSpec((tokens, 2 * head_width), lambda i: (0, i)),
            pl.BlockSpec((2, nope, latent_width), lambda i: (i, 0, 0)),
            pl.BlockSpec((tokens, 2 * value_width), lambda i: (0, i)),
            pl.BlockSpec((2, latent_width, value_width), lambda i: (i, 0, 0)),
        ],
        out_specs=[
            pl.BlockSpec((resp_count, channels, 2 * rows), lambda i: (0, 0, i)),
            pl.BlockSpec((resp_count, latent_width, 2 * rows), lambda i: (0, 0, i)),
        ],
        out_shape=[
            pltpu.HBM((resp_count, channels, heads * rows), BF16),
            pltpu.HBM((resp_count, latent_width, heads * rows), BF16),
        ],
        compiler_params=pltpu.CompilerParams(vmem_limit_bytes=14*1024*1024),
        cost_estimate=pl.CostEstimate(
            flops=4 * tokens * heads * nope * latent_width,
            bytes_accessed=30 * 1024 * 1024,
            transcendentals=0,
        ),
        name="lift_tokens",
    )(*in_hbm(queries, up_key, grad_out, up_value))


def pack_rows(rows):
    slab, channels = rows.shape
    blocks = channels // 128
    half = slab // 2
    tail = jnp.concatenate([rows[:half, 128 * blocks :], rows[half:, 128 * blocks :]], axis=1)
    return jnp.concatenate([rows[:, 128 * c : 128 * (c + 1)] for c in range(blocks)] + [tail], axis=0)


def pack_kernel(axis, prompt_any, latent_any, out_ref, prompt_ref, latent_ref, sem):
    copies = [
        pltpu.make_async_copy(prompt_any, prompt_ref, sem.at[0]),
        pltpu.make_async_copy(latent_any, latent_ref, sem.at[1]),
    ]
    for copy in copies:
        copy.start()
    for copy in copies:
        copy.wait()
    groups, slab_count, packed_rows, lanes = out_ref.shape
    owned = latent_ref.shape[0]
    resp_count = prompt_ref.shape[0] // groups
    first = lax.axis_index(axis) * owned
    packed = [pack_rows(latent_ref[p].astype(F32)).astype(BF16) for p in range(owned)]
    for r in range(groups):
        chosen = packed[0]
        for p in range(1, owned):
            hits = [prompt_ref[r * resp_count + i] == first + p for i in range(resp_count)]
            chosen = jnp.where(functools.reduce(jnp.logical_or, hits), packed[p], chosen)
        out_ref[r] = jnp.broadcast_to(chosen[None], (slab_count, packed_rows, lanes))


def pack(response_prompt, prompt_latent, groups, slab_count):
    owned, slab_rows, channels = prompt_latent.shape
    packed_rows = slab_rows * channels // 128
    return pl.pallas_call(
        functools.partial(pack_kernel, "resp"),
        in_specs=[pl.BlockSpec(memory_space=pl.ANY)] * 2,
        out_specs=pl.BlockSpec(memory_space=pltpu.VMEM),
        scratch_shapes=[
            pltpu.SMEM(response_prompt.shape, response_prompt.dtype),
            pltpu.VMEM(prompt_latent.shape, BF16),
            pltpu.SemaphoreType.DMA((2,)),
        ],
        out_shape=pltpu.VMEM((groups, slab_count, packed_rows, 128), BF16),
        compiler_params=pltpu.CompilerParams(vmem_limit_bytes=10 * 1024 * 1024),
        name="pack",
    )(*in_hbm(response_prompt, prompt_latent))


def own_kernel(head_width, own_ref, fq_ref, gl_ref, e_ref, stat_ref):
    rows = own_ref.shape[0]
    latent_width = gl_ref.shape[1]
    columns = fq_ref.shape[2]
    scaling = LOG2E / math.sqrt(head_width)
    chunk = 2 * rows
    keys = own_ref[...]
    values = keys[:, :latent_width]
    row = lax.broadcasted_iota(jnp.int32, (rows, chunk), 0)
    col = lax.broadcasted_iota(jnp.int32, (rows, chunk), 1) % rows
    allowed = row <= col
    for c in range(columns // chunk):
        at = pl.ds(c * chunk, chunk)
        scores = dot_nn(keys, fq_ref[0, :, at])
        grad_att = dot_nn(values, gl_ref[0, :, at])
        scores = jnp.where(allowed, scores * scaling, -1e30)
        top = jnp.max(scores, axis=0, keepdims=True)
        weights = jnp.exp2(scores - top)
        e_ref[0, :, at] = weights.astype(BF16)
        stat_ref[0, pl.ds(0, 1), at] = top
        stat_ref[0, pl.ds(1, 1), at] = jnp.sum(weights, axis=0, keepdims=True)
        stat_ref[0, pl.ds(2, 1), at] = jnp.sum(weights * grad_att, axis=0, keepdims=True)


def own_scores(resp_latent, full_t, grad_t, head_width):
    resp_count, channels, columns = full_t.shape
    latent_width = grad_t.shape[1]
    rows = resp_latent.shape[0] // resp_count
    return pl.pallas_call(
        functools.partial(own_kernel, head_width),
        grid=(resp_count,),
        in_specs=[
            pl.BlockSpec((rows, channels), lambda j: (j, 0)),
            pl.BlockSpec((1, channels, columns), lambda j: (j, 0, 0)),
            pl.BlockSpec((1, latent_width, columns), lambda j: (j, 0, 0)),
        ],
        out_specs=[
            pl.BlockSpec((1, rows, columns), lambda j: (j, 0, 0)),
            pl.BlockSpec((1, 8, columns), lambda j: (j, 0, 0)),
        ],
        out_shape=[
            pltpu.HBM((resp_count, rows, columns), BF16),
            pltpu.HBM((resp_count, 8, columns), F32),
        ],
        compiler_params=pltpu.CompilerParams(vmem_limit_bytes=10*1024*1024),
        cost_estimate=pl.CostEstimate(
            flops=2 * resp_count * columns * rows * (channels + latent_width),
            bytes_accessed=22 * 1024 * 1024,
            transcendentals=resp_count * columns * rows,
        ),
        name="own_scores",
    )(*in_hbm(resp_latent, full_t, grad_t))


def unpack_latent(packed_ref, slab):
    slabs, packed_rows, lanes = packed_ref.shape[1:]
    return jnp.concatenate(
        [
            jnp.concatenate(
                [packed_ref[0, h, pl.ds(slab * c, slab), :] for h in range(slabs)], axis=0
            )
            for c in range(packed_rows // slab)
        ],
        axis=1,
    )


def unpack_rope(packed_ref, slab):
    slabs, packed_rows, lanes = packed_ref.shape[1:]
    rows = []
    for h in range(slabs):
        tail = packed_ref[0, h].astype(F32)[packed_rows - slab // 2 :]
        rows += [tail[:, : lanes // 2], tail[:, lanes // 2 :]]
    return jnp.concatenate(rows, axis=0).astype(BF16)


def attend_kernel(
    head_width,
    slot_ref,
    len_ref,
    latent_ref,
    stat_ref,
    fq_ref,
    gl_ref,
    aT_ref,
    ratio_ref,
    value_ref,
    piece_ref,
    acc_ref,
    gs_ref,
):
    j = pl.program_id(0)
    channels = fq_ref.shape[1]
    latent_width = gl_ref.shape[1]
    columns = fq_ref.shape[2]
    rope = channels - latent_width
    groups, key_span, _ = acc_ref.shape
    slabs = latent_ref.shape[1]
    slab = key_span // slabs
    scaling = 1.0 / math.sqrt(head_width)
    chunk = 256

    slot = slot_ref[j]
    length = len_ref[j]
    seen = jnp.int32(0)
    for k in range(slot_ref.shape[0]):
        seen = jnp.where((k < j) & (slot_ref[k] == slot), 1, seen)
    values = unpack_latent(latent_ref, slab)
    value_ref[0] = values
    keys_rope = unpack_rope(latent_ref, slab)
    row = lax.broadcasted_iota(jnp.int32, (key_span, chunk), 0)
    allowed = row < length
    for c in range(columns // chunk):
        at = pl.ds(c * chunk, chunk)
        both = jnp.concatenate([fq_ref[0, pl.ds(0, latent_width), at], gl_ref[0, :, at]], axis=1)
        both = dot_nn(values, both)
        rotary = dot_nn(keys_rope, fq_ref[0, pl.ds(latent_width, rope), at])
        scores = both[:, :chunk] + rotary
        grad_att = both[:, chunk:]
        own_top = stat_ref[0, pl.ds(0, 1), at]
        scores = jnp.where(allowed, scores * (scaling * LOG2E), -1e30)
        top = jnp.maximum(jnp.max(scores, axis=0, keepdims=True), own_top)
        weights = jnp.exp2(scores - top)
        shift = jnp.exp2(own_top - top)
        total = jnp.sum(weights, axis=0, keepdims=True) + shift * stat_ref[0, pl.ds(1, 1), at]
        inverse = 1.0 / total
        inner = jnp.sum(weights * grad_att, axis=0, keepdims=True)
        inner = (inner + shift * stat_ref[0, pl.ds(2, 1), at]) * inverse
        aT_ref[0, :, at] = (weights * inverse).astype(BF16)
        gs_ref[:, at] = (weights * (grad_att - inner) * (inverse * scaling)).astype(BF16)
        ratio_ref[0, pl.ds(0, 1), at] = shift * inverse
    combined = dot_nt(gs_ref[...], fq_ref[0])
    value_term = dot_nt(aT_ref[0], gl_ref[0])
    latent_part = combined[:, :latent_width] + value_term
    rope_part = combined[:, latent_width:]
    earlier = acc_ref[slot]
    latent_part += jnp.where(seen == 1, earlier[:, :latent_width], 0.0)
    rope_part += jnp.where(seen == 1, earlier[:, latent_width:], 0.0)
    acc_ref[slot, :, pl.ds(0, latent_width)] = latent_part
    acc_ref[slot, :, pl.ds(latent_width, rope)] = rope_part
    total = jnp.concatenate([latent_part, rope_part], axis=1)
    for h in range(slabs):
        piece_ref[0, h] = pack_rows(total[h * slab : (h + 1) * slab]).astype(BF16)


def attend(slots, lengths, gathered, stats, full_t, grad_t, head_width):
    groups, slabs, packed_rows, lanes = gathered.shape
    resp_count, channels, columns = full_t.shape
    key_span = slabs * packed_rows * lanes // channels
    latent_width = grad_t.shape[1]
    grid_spec = pltpu.PrefetchScalarGridSpec(
        num_scalar_prefetch=2,
        grid=(resp_count,),
        in_specs=[
            pl.BlockSpec((1, slabs, packed_rows, lanes), lambda j, s, n: (s[j], 0, 0, 0)),
            pl.BlockSpec((1, 8, columns), lambda j, s, n: (j, 0, 0)),
            pl.BlockSpec((1, channels, columns), lambda j, s, n: (j, 0, 0)),
            pl.BlockSpec((1, latent_width, columns), lambda j, s, n: (j, 0, 0)),
        ],
        out_specs=[
            pl.BlockSpec((1, key_span, columns), lambda j, s, n: (j, 0, 0)),
            pl.BlockSpec((1, 8, columns), lambda j, s, n: (j, 0, 0)),
            pl.BlockSpec((1, key_span, latent_width), lambda j, s, n: (j, 0, 0)),
            pl.BlockSpec((1, slabs, packed_rows, lanes), lambda j, s, n: (s[j], 0, 0, 0)),
        ],
        scratch_shapes=[
            pltpu.VMEM((groups, key_span, channels), F32),
            pltpu.VMEM((key_span, columns), BF16),
        ],
    )
    return pl.pallas_call(
        functools.partial(attend_kernel, head_width),
        grid_spec=grid_spec,
        out_shape=[
            pltpu.HBM((resp_count, key_span, columns), BF16),
            pltpu.HBM((resp_count, 8, columns), F32),
            pltpu.HBM((resp_count, key_span, latent_width), BF16),
            pltpu.HBM((groups, slabs, packed_rows, lanes), BF16),
        ],
        compiler_params=pltpu.CompilerParams(vmem_limit_bytes=20*1024*1024),
        cost_estimate=pl.CostEstimate(
            flops=2 * resp_count * columns * key_span * 2176,
            bytes_accessed=30 * 1024 * 1024,
            transcendentals=resp_count * columns * key_span,
        ),
        name="attend",
    )(slots, lengths, gathered, *in_hbm(stats, full_t, grad_t))


def output_kernel(latent_ref, own_ref, aT_ref, e_ref, ratio_ref, uv_ref, out_ref):
    rows = own_ref.shape[0]
    heads, latent_width, value_width = uv_ref.shape
    values = jnp.concatenate(
        [latent_ref[0], own_ref[:, pl.ds(0, latent_width)]], axis=0
    )
    values_t = values.T
    for i in range(0, heads, 2):
        at = pl.ds(i * rows, 2 * rows)
        own = (e_ref[0, :, at].astype(F32) * ratio_ref[0, pl.ds(0, 1), at]).astype(BF16)
        weights = jnp.concatenate([aT_ref[0, :, at], own], axis=0)
        latent_t = dot_nn(values_t, weights).astype(BF16)
        for e in range(2):
            part = latent_t[:, e * rows : (e + 1) * rows].T
            done = dot_nn(part, uv_ref[i + e])
            out_ref[:, pl.ds((i + e) * value_width, value_width)] = done.astype(BF16)


def outputs(prompt_values, resp_latent, attention_t, own_weights, ratio, up_value):
    resp_count, key_span, columns = attention_t.shape
    channels = resp_latent.shape[1]
    heads, latent_width, value_width = up_value.shape
    rows = resp_latent.shape[0] // resp_count
    return pl.pallas_call(
        output_kernel,
        grid=(resp_count,),
        in_specs=[
            pl.BlockSpec((1, key_span, latent_width), lambda j: (j, 0, 0)),
            pl.BlockSpec((rows, channels), lambda j: (j, 0)),
            pl.BlockSpec((1, key_span, columns), lambda j: (j, 0, 0)),
            pl.BlockSpec((1, rows, columns), lambda j: (j, 0, 0)),
            pl.BlockSpec((1, 8, columns), lambda j: (j, 0, 0)),
            pl.BlockSpec((heads, latent_width, value_width), lambda j: (0, 0, 0)),
        ],
        out_specs=pl.BlockSpec((rows, heads * value_width), lambda j: (j, 0)),
        out_shape=jax.ShapeDtypeStruct((resp_count * rows, heads * value_width), BF16),
        compiler_params=pltpu.CompilerParams(vmem_limit_bytes=12*1024*1024),
        cost_estimate=pl.CostEstimate(
            flops=2 * resp_count * columns * (384 + 128) * 512,
            bytes_accessed=16 * 1024 * 1024,
            transcendentals=0,
        ),
        name="outputs",
    )(*in_hbm(prompt_values, resp_latent, attention_t, own_weights, ratio, up_value))


def on_device(
    queries, up_key, up_value, prompt_latent, resp_latent, grad_out, response_prompt, prompt_length
):
    groups = lax.axis_size("resp")
    slab_count = lax.axis_size("head")
    my_group = lax.axis_index("resp")
    owned, slab_rows, channels = prompt_latent.shape
    resp_count = response_prompt.shape[0] // groups
    owners = response_prompt // owned
    hit_table = owners[:, None] == jnp.arange(groups)[None, :]
    wanted = jnp.max(
        jnp.where(hit_table, (response_prompt % owned)[:, None], -1).reshape(
            groups, resp_count, groups
        ),
        axis=1,
    )
    wanted_mine = lax.dynamic_index_in_dim(wanted, my_group, 1, False)
    copies = pack(response_prompt, prompt_latent, groups, slab_count)
    copies = copies.reshape(groups * slab_count, -1, 128)
    arrived = lax.all_to_all(copies, ("resp", "head"), split_axis=0, concat_axis=0, tiled=True)
    gathered = arrived.reshape(groups, slab_count, -1, 128)
    local_prompt = lax.dynamic_slice_in_dim(response_prompt, my_group * resp_count, resp_count)
    slots = local_prompt // owned
    hits = local_prompt[:, None] == jnp.arange(prompt_length.shape[0])[None, :]
    lengths = jnp.sum(jnp.where(hits, prompt_length[None, :], 0), axis=1)
    head_width = queries.shape[1] // up_key.shape[0]
    full_t, grad_t = lift_tokens(queries, up_key, grad_out, up_value, resp_count)
    own_weights, stats = own_scores(resp_latent, full_t, grad_t, head_width)
    attention_t, ratio, prompt_values, pieces = attend(
        slots, lengths, gathered, stats, full_t, grad_t, head_width
    )
    returned_grad = lax.all_to_all(
        pieces.reshape(groups * slab_count, -1, 128),
        ("resp", "head"),
        split_axis=0,
        concat_axis=0,
        tiled=True,
    )
    attn_out = outputs(prompt_values, resp_latent, attention_t, own_weights, ratio, up_value)
    summed = jnp.sum(returned_grad.reshape(groups, slab_count, -1, 128).astype(F32), axis=1)
    packed = jnp.stack(
        [
            jnp.sum(jnp.where((wanted_mine == p)[:, None, None], summed, 0.0), axis=0)
            for p in range(owned)
        ]
    )
    blocks = channels // 128
    latent = packed[:, : slab_rows * blocks].reshape(owned, blocks, slab_rows, 128)
    tail = packed[:, slab_rows * blocks :].reshape(owned, slab_rows // 2, 2, 64)
    prompt_grad = jnp.concatenate(
        [
            jnp.transpose(latent, (0, 2, 1, 3)).reshape(owned, slab_rows, blocks * 128),
            jnp.transpose(tail, (0, 2, 1, 3)).reshape(owned, slab_rows, 64),
        ],
        axis=2,
    )
    return (attn_out, prompt_grad)


def solution(mesh):
    return jax.shard_map(
        on_device,
        mesh=mesh,
        in_specs=(
            P("resp", "head"),
            P("head", None, None),
            P("head", None, None),
            P("resp", "head", None),
            P("resp", None),
            P("resp", "head"),
            P(),
            P(),
        ),
        out_specs=(P("resp", "head"), P("resp", "head", None)),
        check_vma=False,
    )
```

```python
import functools
import math

import jax
import jax.numpy as jnp
from jax import lax
from jax.experimental import pallas as pl
from jax.experimental.pallas import tpu as pltpu
from jax.sharding import Mesh, PartitionSpec as P

BF16 = jnp.bfloat16
F32 = jnp.float32
ORDER = ("core", "z", "y", "x")
RESP = ("x", "core")
HEAD = ("y", "z")
LOG2E = 1.4426950408889634


def in_hbm(*arrays):
    return [pltpu.with_memory_space_constraint(a, pltpu.HBM) for a in arrays]


def dot_nn(a, b):
    return lax.dot_general(a, b, (((1,), (0,)), ((), ())), preferred_element_type=F32)


def dot_nt(a, b):
    return lax.dot_general(a, b, (((1,), (1,)), ((), ())), preferred_element_type=F32)


def up_kernel(q_ref, uk_ref, go_ref, uv_ref, fq_ref, gl_ref):
    resp_count, channels, _ = fq_ref.shape
    latent_width = gl_ref.shape[1]
    rope = channels - latent_width
    rows = q_ref.shape[0] // resp_count
    nope = uk_ref.shape[1]
    span = 2 * nope
    for e in range(2):
        lead = e * rope
        lift = uk_ref[e]
        parts = [lift, jnp.zeros((nope - lead, latent_width), BF16)]
        if lead:
            parts = [jnp.zeros((lead, latent_width), BF16)] + parts
        lifted = jnp.concatenate(parts, axis=0).T
        row = lax.broadcasted_iota(jnp.int32, (rope, span), 0)
        col = lax.broadcasted_iota(jnp.int32, (rope, span), 1)
        pick = jnp.where(col == row + (nope + lead), 1.0, 0.0).astype(BF16)
        up_value = uv_ref[e]
        for j in range(0, resp_count, 2):
            window = q_ref[pl.ds(j * rows, 2 * rows), pl.ds(e * nope, span)]
            grad = go_ref[pl.ds(j * rows, 2 * rows), pl.ds(e * rows, rows)]
            top = dot_nt(lifted, window).astype(BF16)
            low = dot_nt(pick, window).astype(BF16)
            lat = dot_nt(up_value, grad).astype(BF16)
            for i in range(2):
                src = slice(i * rows, (i + 1) * rows)
                dst = pl.ds(e * rows, rows)
                fq_ref[j + i, pl.ds(0, latent_width), dst] = top[:, src]
                fq_ref[j + i, pl.ds(latent_width, rope), dst] = low[:, src]
                gl_ref[j + i, :, dst] = lat[:, src]


def lift_tokens(queries, up_key, grad_out, up_value, resp_count):
    tokens = queries.shape[0]
    rows = tokens // resp_count
    heads, nope, latent_width = up_key.shape
    value_width = up_value.shape[2]
    head_width = queries.shape[1] // heads
    channels = latent_width + head_width - nope
    return pl.pallas_call(
        up_kernel,
        grid=(heads // 2,),
        in_specs=[
            pl.BlockSpec((tokens, 2 * head_width), lambda i: (0, i)),
            pl.BlockSpec((2, nope, latent_width), lambda i: (i, 0, 0)),
            pl.BlockSpec((tokens, 2 * value_width), lambda i: (0, i)),
            pl.BlockSpec((2, latent_width, value_width), lambda i: (i, 0, 0)),
        ],
        out_specs=[
            pl.BlockSpec((resp_count, channels, 2 * rows), lambda i: (0, 0, i)),
            pl.BlockSpec((resp_count, latent_width, 2 * rows), lambda i: (0, 0, i)),
        ],
        out_shape=[
            pltpu.HBM((resp_count, channels, heads * rows), BF16),
            pltpu.HBM((resp_count, latent_width, heads * rows), BF16),
        ],
        compiler_params=pltpu.CompilerParams(vmem_limit_bytes=14*1024*1024),
        cost_estimate=pl.CostEstimate(
            flops=4 * tokens * heads * nope * latent_width,
            bytes_accessed=30 * 1024 * 1024,
            transcendentals=0,
        ),
        name="lift_tokens",
    )(*in_hbm(queries, up_key, grad_out, up_value))


def pack_rows(rows):
    slab, channels = rows.shape
    blocks = channels // 128
    half = slab // 2
    tail = jnp.concatenate([rows[:half, 128 * blocks :], rows[half:, 128 * blocks :]], axis=1)
    return jnp.concatenate([rows[:, 128 * c : 128 * (c + 1)] for c in range(blocks)] + [tail], axis=0)


def pack_kernel(axis, prompt_any, latent_any, out_ref, prompt_ref, latent_ref, sem):
    copies = [
        pltpu.make_async_copy(prompt_any, prompt_ref, sem.at[0]),
        pltpu.make_async_copy(latent_any, latent_ref, sem.at[1]),
    ]
    for copy in copies:
        copy.start()
    for copy in copies:
        copy.wait()
    cores, depth, height, width, packed_rows, lanes = out_ref.shape
    groups = cores * width
    owned = latent_ref.shape[0]
    resp_count = prompt_ref.shape[0] // groups
    first = lax.axis_index(axis) * owned
    packed = [pack_rows(latent_ref[p].astype(F32)).astype(BF16) for p in range(owned)]
    for r in range(groups):
        chosen = packed[0]
        for p in range(1, owned):
            hits = [prompt_ref[r * resp_count + i] == first + p for i in range(resp_count)]
            chosen = jnp.where(functools.reduce(jnp.logical_or, hits), packed[p], chosen)
        out_ref[r % cores, :, :, r // cores] = jnp.broadcast_to(
            chosen[None, None], (depth, height, packed_rows, lanes)
        )


def pack(response_prompt, prompt_latent, extents):
    owned, slab_rows, channels = prompt_latent.shape
    packed_rows = slab_rows * channels // 128
    return pl.pallas_call(
        functools.partial(pack_kernel, RESP),
        in_specs=[pl.BlockSpec(memory_space=pl.ANY)] * 2,
        out_specs=pl.BlockSpec(memory_space=pltpu.VMEM),
        scratch_shapes=[
            pltpu.SMEM(response_prompt.shape, response_prompt.dtype),
            pltpu.VMEM(prompt_latent.shape, BF16),
            pltpu.SemaphoreType.DMA((2,)),
        ],
        out_shape=pltpu.VMEM(extents + (packed_rows, 128), BF16),
        compiler_params=pltpu.CompilerParams(vmem_limit_bytes=10 * 1024 * 1024),
        name="pack",
    )(*in_hbm(response_prompt, prompt_latent))


def own_kernel(head_width, own_ref, fq_ref, gl_ref, e_ref, stat_ref):
    rows = own_ref.shape[0]
    latent_width = gl_ref.shape[1]
    columns = fq_ref.shape[2]
    scaling = LOG2E / math.sqrt(head_width)
    chunk = 2 * rows
    keys = own_ref[...]
    values = keys[:, :latent_width]
    row = lax.broadcasted_iota(jnp.int32, (rows, chunk), 0)
    col = lax.broadcasted_iota(jnp.int32, (rows, chunk), 1) % rows
    allowed = row <= col
    for c in range(columns // chunk):
        at = pl.ds(c * chunk, chunk)
        scores = dot_nn(keys, fq_ref[0, :, at])
        grad_att = dot_nn(values, gl_ref[0, :, at])
        scores = jnp.where(allowed, scores * scaling, -1e30)
        top = jnp.max(scores, axis=0, keepdims=True)
        weights = jnp.exp2(scores - top)
        e_ref[0, :, at] = weights.astype(BF16)
        stat_ref[0, pl.ds(0, 1), at] = top
        stat_ref[0, pl.ds(1, 1), at] = jnp.sum(weights, axis=0, keepdims=True)
        stat_ref[0, pl.ds(2, 1), at] = jnp.sum(weights * grad_att, axis=0, keepdims=True)


def own_scores(resp_latent, full_t, grad_t, head_width):
    resp_count, channels, columns = full_t.shape
    latent_width = grad_t.shape[1]
    rows = resp_latent.shape[0] // resp_count
    return pl.pallas_call(
        functools.partial(own_kernel, head_width),
        grid=(resp_count,),
        in_specs=[
            pl.BlockSpec((rows, channels), lambda j: (j, 0)),
            pl.BlockSpec((1, channels, columns), lambda j: (j, 0, 0)),
            pl.BlockSpec((1, latent_width, columns), lambda j: (j, 0, 0)),
        ],
        out_specs=[
            pl.BlockSpec((1, rows, columns), lambda j: (j, 0, 0)),
            pl.BlockSpec((1, 8, columns), lambda j: (j, 0, 0)),
        ],
        out_shape=[
            pltpu.HBM((resp_count, rows, columns), BF16),
            pltpu.HBM((resp_count, 8, columns), F32),
        ],
        compiler_params=pltpu.CompilerParams(vmem_limit_bytes=10*1024*1024),
        cost_estimate=pl.CostEstimate(
            flops=2 * resp_count * columns * rows * (channels + latent_width),
            bytes_accessed=22 * 1024 * 1024,
            transcendentals=resp_count * columns * rows,
        ),
        name="own_scores",
    )(*in_hbm(resp_latent, full_t, grad_t))


def slab_list(ref):
    _, depth, height, _, packed_rows, _ = ref.shape
    return [(0, z, y, 0) for y in range(height) for z in range(depth)], packed_rows


def unpack_latent(packed_ref, slab):
    places, packed_rows = slab_list(packed_ref)
    return jnp.concatenate(
        [
            jnp.concatenate([packed_ref[p + (pl.ds(slab * c, slab),)] for p in places], axis=0)
            for c in range(packed_rows // slab)
        ],
        axis=1,
    )


def unpack_rope(packed_ref, slab):
    places, packed_rows = slab_list(packed_ref)
    rows = []
    for p in places:
        tail = packed_ref[p].astype(F32)[packed_rows - slab // 2 :]
        half = tail.shape[1] // 2
        rows += [tail[:, :half], tail[:, half:]]
    return jnp.concatenate(rows, axis=0).astype(BF16)


def attend_kernel(
    head_width,
    slot_ref,
    len_ref,
    latent_ref,
    stat_ref,
    fq_ref,
    gl_ref,
    aT_ref,
    ratio_ref,
    value_ref,
    piece_ref,
    acc_ref,
    gs_ref,
):
    j = pl.program_id(0)
    channels = fq_ref.shape[1]
    latent_width = gl_ref.shape[1]
    columns = fq_ref.shape[2]
    rope = channels - latent_width
    groups, key_span, _ = acc_ref.shape
    places, _ = slab_list(latent_ref)
    slab = key_span // len(places)
    scaling = 1.0 / math.sqrt(head_width)
    chunk = 256

    slot = slot_ref[j]
    length = len_ref[j]
    seen = jnp.int32(0)
    for k in range(slot_ref.shape[0]):
        seen = jnp.where((k < j) & (slot_ref[k] == slot), 1, seen)
    values = unpack_latent(latent_ref, slab)
    value_ref[0] = values
    keys_rope = unpack_rope(latent_ref, slab)
    row = lax.broadcasted_iota(jnp.int32, (key_span, chunk), 0)
    allowed = row < length
    for c in range(columns // chunk):
        at = pl.ds(c * chunk, chunk)
        both = jnp.concatenate([fq_ref[0, pl.ds(0, latent_width), at], gl_ref[0, :, at]], axis=1)
        both = dot_nn(values, both)
        rotary = dot_nn(keys_rope, fq_ref[0, pl.ds(latent_width, rope), at])
        scores = both[:, :chunk] + rotary
        grad_att = both[:, chunk:]
        own_top = stat_ref[0, pl.ds(0, 1), at]
        scores = jnp.where(allowed, scores * (scaling * LOG2E), -1e30)
        top = jnp.maximum(jnp.max(scores, axis=0, keepdims=True), own_top)
        weights = jnp.exp2(scores - top)
        shift = jnp.exp2(own_top - top)
        total = jnp.sum(weights, axis=0, keepdims=True) + shift * stat_ref[0, pl.ds(1, 1), at]
        inverse = 1.0 / total
        inner = jnp.sum(weights * grad_att, axis=0, keepdims=True)
        inner = (inner + shift * stat_ref[0, pl.ds(2, 1), at]) * inverse
        aT_ref[0, :, at] = (weights * inverse).astype(BF16)
        gs_ref[:, at] = (weights * (grad_att - inner) * (inverse * scaling)).astype(BF16)
        ratio_ref[0, pl.ds(0, 1), at] = shift * inverse
    combined = dot_nt(gs_ref[...], fq_ref[0])
    value_term = dot_nt(aT_ref[0], gl_ref[0])
    latent_part = combined[:, :latent_width] + value_term
    rope_part = combined[:, latent_width:]
    earlier = acc_ref[slot]
    latent_part += jnp.where(seen == 1, earlier[:, :latent_width], 0.0)
    rope_part += jnp.where(seen == 1, earlier[:, latent_width:], 0.0)
    acc_ref[slot, :, pl.ds(0, latent_width)] = latent_part
    acc_ref[slot, :, pl.ds(latent_width, rope)] = rope_part
    total = jnp.concatenate([latent_part, rope_part], axis=1)
    for h, place in enumerate(places):
        piece_ref[place] = pack_rows(total[h * slab : (h + 1) * slab]).astype(BF16)


def attend(slots, lengths, gathered, stats, full_t, grad_t, head_width):
    cores, depth, height, width, packed_rows, lanes = gathered.shape
    groups = cores * width
    resp_count, channels, columns = full_t.shape
    key_span = depth * height * packed_rows * lanes // channels
    block = (1, depth, height, 1, packed_rows, lanes)

    def slot_block(j, s, n):
        return (lax.rem(s[j], cores), 0, 0, lax.div(s[j], cores), 0, 0)

    latent_width = grad_t.shape[1]
    grid_spec = pltpu.PrefetchScalarGridSpec(
        num_scalar_prefetch=2,
        grid=(resp_count,),
        in_specs=[
            pl.BlockSpec(block, slot_block),
            pl.BlockSpec((1, 8, columns), lambda j, s, n: (j, 0, 0)),
            pl.BlockSpec((1, channels, columns), lambda j, s, n: (j, 0, 0)),
            pl.BlockSpec((1, latent_width, columns), lambda j, s, n: (j, 0, 0)),
        ],
        out_specs=[
            pl.BlockSpec((1, key_span, columns), lambda j, s, n: (j, 0, 0)),
            pl.BlockSpec((1, 8, columns), lambda j, s, n: (j, 0, 0)),
            pl.BlockSpec((1, key_span, latent_width), lambda j, s, n: (j, 0, 0)),
            pl.BlockSpec(block, slot_block),
        ],
        scratch_shapes=[
            pltpu.VMEM((groups, key_span, channels), F32),
            pltpu.VMEM((key_span, columns), BF16),
        ],
    )
    return pl.pallas_call(
        functools.partial(attend_kernel, head_width),
        grid_spec=grid_spec,
        out_shape=[
            pltpu.HBM((resp_count, key_span, columns), BF16),
            pltpu.HBM((resp_count, 8, columns), F32),
            pltpu.HBM((resp_count, key_span, latent_width), BF16),
            pltpu.HBM(gathered.shape, BF16),
        ],
        compiler_params=pltpu.CompilerParams(vmem_limit_bytes=20*1024*1024),
        cost_estimate=pl.CostEstimate(
            flops=2 * resp_count * columns * key_span * 2176,
            bytes_accessed=30 * 1024 * 1024,
            transcendentals=resp_count * columns * key_span,
        ),
        name="attend",
    )(slots, lengths, gathered, *in_hbm(stats, full_t, grad_t))


def output_kernel(latent_ref, own_ref, aT_ref, e_ref, ratio_ref, uv_ref, out_ref):
    rows = own_ref.shape[0]
    heads, latent_width, value_width = uv_ref.shape
    values = jnp.concatenate(
        [latent_ref[0], own_ref[:, pl.ds(0, latent_width)]], axis=0
    )
    values_t = values.T
    for i in range(0, heads, 2):
        at = pl.ds(i * rows, 2 * rows)
        own = (e_ref[0, :, at].astype(F32) * ratio_ref[0, pl.ds(0, 1), at]).astype(BF16)
        weights = jnp.concatenate([aT_ref[0, :, at], own], axis=0)
        latent_t = dot_nn(values_t, weights).astype(BF16)
        for e in range(2):
            part = latent_t[:, e * rows : (e + 1) * rows].T
            done = dot_nn(part, uv_ref[i + e])
            out_ref[:, pl.ds((i + e) * value_width, value_width)] = done.astype(BF16)


def outputs(prompt_values, resp_latent, attention_t, own_weights, ratio, up_value):
    resp_count, key_span, columns = attention_t.shape
    channels = resp_latent.shape[1]
    heads, latent_width, value_width = up_value.shape
    rows = resp_latent.shape[0] // resp_count
    return pl.pallas_call(
        output_kernel,
        grid=(resp_count,),
        in_specs=[
            pl.BlockSpec((1, key_span, latent_width), lambda j: (j, 0, 0)),
            pl.BlockSpec((rows, channels), lambda j: (j, 0)),
            pl.BlockSpec((1, key_span, columns), lambda j: (j, 0, 0)),
            pl.BlockSpec((1, rows, columns), lambda j: (j, 0, 0)),
            pl.BlockSpec((1, 8, columns), lambda j: (j, 0, 0)),
            pl.BlockSpec((heads, latent_width, value_width), lambda j: (0, 0, 0)),
        ],
        out_specs=pl.BlockSpec((rows, heads * value_width), lambda j: (j, 0)),
        out_shape=jax.ShapeDtypeStruct((resp_count * rows, heads * value_width), BF16),
        compiler_params=pltpu.CompilerParams(vmem_limit_bytes=12*1024*1024),
        cost_estimate=pl.CostEstimate(
            flops=2 * resp_count * columns * (384 + 128) * 512,
            bytes_accessed=16 * 1024 * 1024,
            transcendentals=0,
        ),
        name="outputs",
    )(*in_hbm(prompt_values, resp_latent, attention_t, own_weights, ratio, up_value))


def on_device(
    queries, up_key, up_value, prompt_latent, resp_latent, grad_out, response_prompt, prompt_length
):
    extents = tuple(lax.axis_size(name) for name in ORDER)
    cores, _, _, width = extents
    groups = cores * width
    my_group = lax.axis_index(RESP)
    owned, slab_rows, channels = prompt_latent.shape
    resp_count = response_prompt.shape[0] // groups
    owners = response_prompt // owned
    hit_table = owners[:, None] == jnp.arange(groups)[None, :]
    wanted = jnp.max(
        jnp.where(hit_table, (response_prompt % owned)[:, None], -1).reshape(
            groups, resp_count, groups
        ),
        axis=1,
    )
    wanted_mine = lax.dynamic_index_in_dim(wanted, my_group, 1, False)
    copies = pack(response_prompt, prompt_latent, extents)
    arrived = lax.all_to_all(
        copies.reshape((-1,) + copies.shape[4:]), ORDER, split_axis=0, concat_axis=0, tiled=True
    )
    gathered = arrived.reshape(copies.shape)
    local_prompt = lax.dynamic_slice_in_dim(response_prompt, my_group * resp_count, resp_count)
    slots = local_prompt // owned
    hits = local_prompt[:, None] == jnp.arange(prompt_length.shape[0])[None, :]
    lengths = jnp.sum(jnp.where(hits, prompt_length[None, :], 0), axis=1)
    head_width = queries.shape[1] // up_key.shape[0]
    full_t, grad_t = lift_tokens(queries, up_key, grad_out, up_value, resp_count)
    own_weights, stats = own_scores(resp_latent, full_t, grad_t, head_width)
    attention_t, ratio, prompt_values, pieces = attend(
        slots, lengths, gathered, stats, full_t, grad_t, head_width
    )
    returned_grad = lax.all_to_all(
        pieces.reshape((-1,) + pieces.shape[4:]), ORDER, split_axis=0, concat_axis=0, tiled=True
    )
    attn_out = outputs(prompt_values, resp_latent, attention_t, own_weights, ratio, up_value)
    summed = jnp.sum(returned_grad.reshape(pieces.shape).astype(F32), axis=(1, 2))
    kept = wanted_mine.reshape(width, cores).T[:, :, None, None]
    packed = jnp.stack(
        [jnp.sum(jnp.where(kept == p, summed, 0.0), axis=(0, 1)) for p in range(owned)]
    )
    blocks = channels // 128
    latent = packed[:, : slab_rows * blocks].reshape(owned, blocks, slab_rows, 128)
    tail = packed[:, slab_rows * blocks :].reshape(owned, slab_rows // 2, 2, 64)
    prompt_grad = jnp.concatenate(
        [
            jnp.transpose(latent, (0, 2, 1, 3)).reshape(owned, slab_rows, blocks * 128),
            jnp.transpose(tail, (0, 2, 1, 3)).reshape(owned, slab_rows, 64),
        ],
        axis=2,
    )
    return (attn_out, prompt_grad)


def solution(mesh):
    groups, slab_count = mesh.devices.shape
    devices = mesh.devices.reshape(groups // 2, 2, slab_count // 4, 4)
    return jax.shard_map(
        on_device,
        mesh=Mesh(devices, RESP + HEAD),
        in_specs=(
            P(RESP, HEAD),
            P(HEAD, None, None),
            P(HEAD, None, None),
            P(RESP, HEAD, None),
            P(RESP, None),
            P(RESP, HEAD),
            P(),
            P(),
        ),
        out_specs=(P(RESP, HEAD), P(RESP, HEAD, None)),
        check_vma=False,
    )
```

```python
import functools
import math

import jax
import jax.numpy as jnp
from jax import lax
from jax.experimental import pallas as pl
from jax.experimental.pallas import tpu as pltpu
from jax.sharding import Mesh, PartitionSpec as P

BF16 = jnp.bfloat16
F32 = jnp.float32
ORDER = ("core", "z", "y", "x")
RESP = ("x", "core")
HEAD = ("y", "z")
LOG2E = 1.4426950408889634


def in_hbm(*arrays):
    return [pltpu.with_memory_space_constraint(a, pltpu.HBM) for a in arrays]


def dot_nn(a, b):
    return lax.dot_general(a, b, (((1,), (0,)), ((), ())), preferred_element_type=F32)


def dot_nt(a, b):
    return lax.dot_general(a, b, (((1,), (1,)), ((), ())), preferred_element_type=F32)


def up_kernel(q_ref, uk_ref, go_ref, uv_ref, fq_ref, gl_ref):
    resp_count, channels, _ = fq_ref.shape
    latent_width = gl_ref.shape[1]
    rope = channels - latent_width
    rows = q_ref.shape[0] // resp_count
    nope = uk_ref.shape[1]
    span = 2 * nope
    for e in range(2):
        lead = e * rope
        lift = uk_ref[e]
        parts = [lift, jnp.zeros((nope - lead, latent_width), BF16)]
        if lead:
            parts = [jnp.zeros((lead, latent_width), BF16)] + parts
        lifted = jnp.concatenate(parts, axis=0).T
        row = lax.broadcasted_iota(jnp.int32, (rope, span), 0)
        col = lax.broadcasted_iota(jnp.int32, (rope, span), 1)
        pick = jnp.where(col == row + (nope + lead), 1.0, 0.0).astype(BF16)
        up_value = uv_ref[e]
        for j in range(0, resp_count, 2):
            window = q_ref[pl.ds(j * rows, 2 * rows), pl.ds(e * nope, span)]
            grad = go_ref[pl.ds(j * rows, 2 * rows), pl.ds(e * rows, rows)]
            top = dot_nt(lifted, window).astype(BF16)
            low = dot_nt(pick, window).astype(BF16)
            lat = dot_nt(up_value, grad).astype(BF16)
            for i in range(2):
                src = slice(i * rows, (i + 1) * rows)
                dst = pl.ds(e * rows, rows)
                fq_ref[j + i, pl.ds(0, latent_width), dst] = top[:, src]
                fq_ref[j + i, pl.ds(latent_width, rope), dst] = low[:, src]
                gl_ref[j + i, :, dst] = lat[:, src]


def lift_tokens(queries, up_key, grad_out, up_value, resp_count):
    tokens = queries.shape[0]
    rows = tokens // resp_count
    heads, nope, latent_width = up_key.shape
    value_width = up_value.shape[2]
    head_width = queries.shape[1] // heads
    channels = latent_width + head_width - nope
    return pl.pallas_call(
        up_kernel,
        grid=(heads // 2,),
        in_specs=[
            pl.BlockSpec((tokens, 2 * head_width), lambda i: (0, i)),
            pl.BlockSpec((2, nope, latent_width), lambda i: (i, 0, 0)),
            pl.BlockSpec((tokens, 2 * value_width), lambda i: (0, i)),
            pl.BlockSpec((2, latent_width, value_width), lambda i: (i, 0, 0)),
        ],
        out_specs=[
            pl.BlockSpec((resp_count, channels, 2 * rows), lambda i: (0, 0, i)),
            pl.BlockSpec((resp_count, latent_width, 2 * rows), lambda i: (0, 0, i)),
        ],
        out_shape=[
            pltpu.HBM((resp_count, channels, heads * rows), BF16),
            pltpu.HBM((resp_count, latent_width, heads * rows), BF16),
        ],
        compiler_params=pltpu.CompilerParams(vmem_limit_bytes=14*1024*1024),
        cost_estimate=pl.CostEstimate(
            flops=4 * tokens * heads * nope * latent_width,
            bytes_accessed=30 * 1024 * 1024,
            transcendentals=0,
        ),
        name="lift_tokens",
    )(*in_hbm(queries, up_key, grad_out, up_value))


def pack_rows(rows):
    slab, channels = rows.shape
    blocks = channels // 128
    half = slab // 2
    tail = jnp.concatenate([rows[:half, 128 * blocks :], rows[half:, 128 * blocks :]], axis=1)
    return jnp.concatenate([rows[:, 128 * c : 128 * (c + 1)] for c in range(blocks)] + [tail], axis=0)


def pack_kernel(
    axis, prompt_any, latent_any, out_ref, prompt_ref, latent_ref, block_ref, sem, out_sem
):
    copies = [
        pltpu.make_async_copy(prompt_any, prompt_ref, sem.at[0]),
        pltpu.make_async_copy(latent_any, latent_ref, sem.at[1]),
    ]
    for copy in copies:
        copy.start()
    for copy in copies:
        copy.wait()
    cores, depth, height, width, packed_rows, lanes = out_ref.shape
    groups = cores * width
    owned = latent_ref.shape[0]
    resp_count = prompt_ref.shape[0] // groups
    first = lax.axis_index(axis) * owned
    packed = [pack_rows(latent_ref[p].astype(F32)).astype(BF16) for p in range(owned)]
    sends = []
    for r in range(groups):
        chosen = packed[0]
        for p in range(1, owned):
            hits = [prompt_ref[r * resp_count + i] == first + p for i in range(resp_count)]
            chosen = jnp.where(functools.reduce(jnp.logical_or, hits), packed[p], chosen)
        block_ref[r] = jnp.broadcast_to(
            chosen[None, None], (depth, height, packed_rows, lanes)
        )
        sends.append(
            pltpu.make_async_copy(
                block_ref.at[r], out_ref.at[r % cores, :, :, r // cores], out_sem.at[r]
            )
        )
        sends[r].start()
    for send in sends:
        send.wait()


def pack(response_prompt, prompt_latent, extents):
    owned, slab_rows, channels = prompt_latent.shape
    packed_rows = slab_rows * channels // 128
    groups = extents[0] * extents[3]
    return pl.pallas_call(
        functools.partial(pack_kernel, RESP),
        in_specs=[pl.BlockSpec(memory_space=pl.ANY)] * 2,
        out_specs=pl.BlockSpec(memory_space=pl.ANY),
        scratch_shapes=[
            pltpu.SMEM(response_prompt.shape, response_prompt.dtype),
            pltpu.VMEM(prompt_latent.shape, BF16),
            pltpu.VMEM((groups,) + extents[1:3] + (packed_rows, 128), BF16),
            pltpu.SemaphoreType.DMA((2,)),
            pltpu.SemaphoreType.DMA((groups,)),
        ],
        out_shape=pltpu.HBM(extents + (packed_rows, 128), BF16),
        compiler_params=pltpu.CompilerParams(vmem_limit_bytes=10 * 1024 * 1024),
        name="pack",
    )(*in_hbm(response_prompt, prompt_latent))


def own_kernel(head_width, own_ref, fq_ref, gl_ref, e_ref, stat_ref):
    rows = own_ref.shape[0]
    latent_width = gl_ref.shape[1]
    columns = fq_ref.shape[2]
    scaling = LOG2E / math.sqrt(head_width)
    chunk = 2 * rows
    keys = own_ref[...]
    values = keys[:, :latent_width]
    row = lax.broadcasted_iota(jnp.int32, (rows, chunk), 0)
    col = lax.broadcasted_iota(jnp.int32, (rows, chunk), 1) % rows
    allowed = row <= col
    for c in range(columns // chunk):
        at = pl.ds(c * chunk, chunk)
        scores = dot_nn(keys, fq_ref[0, :, at])
        grad_att = dot_nn(values, gl_ref[0, :, at])
        scores = jnp.where(allowed, scores * scaling, -1e30)
        top = jnp.max(scores, axis=0, keepdims=True)
        weights = jnp.exp2(scores - top)
        e_ref[0, :, at] = weights.astype(BF16)
        stat_ref[0, pl.ds(0, 1), at] = top
        stat_ref[0, pl.ds(1, 1), at] = jnp.sum(weights, axis=0, keepdims=True)
        stat_ref[0, pl.ds(2, 1), at] = jnp.sum(weights * grad_att, axis=0, keepdims=True)


def own_scores(resp_latent, full_t, grad_t, head_width):
    resp_count, channels, columns = full_t.shape
    latent_width = grad_t.shape[1]
    rows = resp_latent.shape[0] // resp_count
    return pl.pallas_call(
        functools.partial(own_kernel, head_width),
        grid=(resp_count,),
        in_specs=[
            pl.BlockSpec((rows, channels), lambda j: (j, 0)),
            pl.BlockSpec((1, channels, columns), lambda j: (j, 0, 0)),
            pl.BlockSpec((1, latent_width, columns), lambda j: (j, 0, 0)),
        ],
        out_specs=[
            pl.BlockSpec((1, rows, columns), lambda j: (j, 0, 0)),
            pl.BlockSpec((1, 8, columns), lambda j: (j, 0, 0)),
        ],
        out_shape=[
            pltpu.HBM((resp_count, rows, columns), BF16),
            pltpu.HBM((resp_count, 8, columns), F32),
        ],
        compiler_params=pltpu.CompilerParams(vmem_limit_bytes=10*1024*1024),
        cost_estimate=pl.CostEstimate(
            flops=2 * resp_count * columns * rows * (channels + latent_width),
            bytes_accessed=22 * 1024 * 1024,
            transcendentals=resp_count * columns * rows,
        ),
        name="own_scores",
    )(*in_hbm(resp_latent, full_t, grad_t))


def slab_list(ref):
    _, depth, height, _, packed_rows, _ = ref.shape
    return [(0, z, y, 0) for y in range(height) for z in range(depth)], packed_rows


def unpack_latent(packed_ref, slab):
    places, packed_rows = slab_list(packed_ref)
    return jnp.concatenate(
        [
            jnp.concatenate([packed_ref[p + (pl.ds(slab * c, slab),)] for p in places], axis=0)
            for c in range(packed_rows // slab)
        ],
        axis=1,
    )


def unpack_rope(packed_ref, slab):
    places, packed_rows = slab_list(packed_ref)
    rows = []
    for p in places:
        tail = packed_ref[p].astype(F32)[packed_rows - slab // 2 :]
        half = tail.shape[1] // 2
        rows += [tail[:, :half], tail[:, half:]]
    return jnp.concatenate(rows, axis=0).astype(BF16)


def attend_kernel(
    head_width,
    slot_ref,
    len_ref,
    latent_ref,
    stat_ref,
    fq_ref,
    gl_ref,
    aT_ref,
    ratio_ref,
    value_ref,
    piece_ref,
    acc_ref,
    gs_ref,
):
    j = pl.program_id(0)
    channels = fq_ref.shape[1]
    latent_width = gl_ref.shape[1]
    columns = fq_ref.shape[2]
    rope = channels - latent_width
    groups, key_span, _ = acc_ref.shape
    places, _ = slab_list(latent_ref)
    slab = key_span // len(places)
    scaling = 1.0 / math.sqrt(head_width)
    chunk = 256

    slot = slot_ref[j]
    length = len_ref[j]
    seen = jnp.int32(0)
    for k in range(slot_ref.shape[0]):
        seen = jnp.where((k < j) & (slot_ref[k] == slot), 1, seen)
    values = unpack_latent(latent_ref, slab)
    value_ref[0] = values
    keys_rope = unpack_rope(latent_ref, slab)
    row = lax.broadcasted_iota(jnp.int32, (key_span, chunk), 0)
    allowed = row < length
    for c in range(columns // chunk):
        at = pl.ds(c * chunk, chunk)
        both = jnp.concatenate([fq_ref[0, pl.ds(0, latent_width), at], gl_ref[0, :, at]], axis=1)
        both = dot_nn(values, both)
        rotary = dot_nn(keys_rope, fq_ref[0, pl.ds(latent_width, rope), at])
        scores = both[:, :chunk] + rotary
        grad_att = both[:, chunk:]
        own_top = stat_ref[0, pl.ds(0, 1), at]
        scores = jnp.where(allowed, scores * (scaling * LOG2E), -1e30)
        top = jnp.maximum(jnp.max(scores, axis=0, keepdims=True), own_top)
        weights = jnp.exp2(scores - top)
        shift = jnp.exp2(own_top - top)
        total = jnp.sum(weights, axis=0, keepdims=True) + shift * stat_ref[0, pl.ds(1, 1), at]
        inverse = 1.0 / total
        inner = jnp.sum(weights * grad_att, axis=0, keepdims=True)
        inner = (inner + shift * stat_ref[0, pl.ds(2, 1), at]) * inverse
        gs_ref[:, at] = (weights * (grad_att - inner) * (inverse * scaling)).astype(BF16)
        aT_ref[0, :, at] = (weights * inverse).astype(BF16)
        ratio_ref[0, pl.ds(0, 1), at] = shift * inverse
    combined = dot_nt(gs_ref[...], fq_ref[0])
    value_term = dot_nt(aT_ref[0], gl_ref[0])
    latent_part = combined[:, :latent_width] + value_term
    rope_part = combined[:, latent_width:]
    earlier = acc_ref[slot]
    latent_part += jnp.where(seen == 1, earlier[:, :latent_width], 0.0)
    rope_part += jnp.where(seen == 1, earlier[:, latent_width:], 0.0)
    acc_ref[slot, :, pl.ds(0, latent_width)] = latent_part
    acc_ref[slot, :, pl.ds(latent_width, rope)] = rope_part
    total = jnp.concatenate([latent_part, rope_part], axis=1)
    for h, place in enumerate(places):
        piece_ref[place] = pack_rows(total[h * slab : (h + 1) * slab]).astype(BF16)


def attend(slots, lengths, gathered, stats, full_t, grad_t, head_width):
    cores, depth, height, width, packed_rows, lanes = gathered.shape
    groups = cores * width
    resp_count, channels, columns = full_t.shape
    key_span = depth * height * packed_rows * lanes // channels
    block = (1, depth, height, 1, packed_rows, lanes)

    def slot_block(j, s, n):
        return (lax.rem(s[j], cores), 0, 0, lax.div(s[j], cores), 0, 0)

    latent_width = grad_t.shape[1]
    grid_spec = pltpu.PrefetchScalarGridSpec(
        num_scalar_prefetch=2,
        grid=(resp_count,),
        in_specs=[
            pl.BlockSpec(block, slot_block),
            pl.BlockSpec((1, 8, columns), lambda j, s, n: (j, 0, 0)),
            pl.BlockSpec((1, channels, columns), lambda j, s, n: (j, 0, 0)),
            pl.BlockSpec((1, latent_width, columns), lambda j, s, n: (j, 0, 0)),
        ],
        out_specs=[
            pl.BlockSpec((1, key_span, columns), lambda j, s, n: (j, 0, 0)),
            pl.BlockSpec((1, 8, columns), lambda j, s, n: (j, 0, 0)),
            pl.BlockSpec((1, key_span, latent_width), lambda j, s, n: (j, 0, 0)),
            pl.BlockSpec(block, slot_block),
        ],
        scratch_shapes=[
            pltpu.VMEM((groups, key_span, channels), F32),
            pltpu.VMEM((key_span, columns), BF16),
        ],
    )
    return pl.pallas_call(
        functools.partial(attend_kernel, head_width),
        grid_spec=grid_spec,
        out_shape=[
            pltpu.HBM((resp_count, key_span, columns), BF16),
            pltpu.HBM((resp_count, 8, columns), F32),
            pltpu.HBM((resp_count, key_span, latent_width), BF16),
            pltpu.HBM(gathered.shape, BF16),
        ],
        compiler_params=pltpu.CompilerParams(vmem_limit_bytes=20*1024*1024),
        cost_estimate=pl.CostEstimate(
            flops=2 * resp_count * columns * key_span * 2176,
            bytes_accessed=30 * 1024 * 1024,
            transcendentals=resp_count * columns * key_span,
        ),
        name="attend",
    )(slots, lengths, gathered, *in_hbm(stats, full_t, grad_t))


def output_kernel(latent_ref, own_ref, aT_ref, e_ref, ratio_ref, uv_ref, out_ref):
    rows = own_ref.shape[0]
    heads, latent_width, value_width = uv_ref.shape
    values = jnp.concatenate(
        [latent_ref[0], own_ref[:, pl.ds(0, latent_width)]], axis=0
    )
    values_t = values.T
    for i in range(0, heads, 2):
        at = pl.ds(i * rows, 2 * rows)
        own = (e_ref[0, :, at].astype(F32) * ratio_ref[0, pl.ds(0, 1), at]).astype(BF16)
        weights = jnp.concatenate([aT_ref[0, :, at], own], axis=0)
        latent_t = dot_nn(values_t, weights).astype(BF16)
        for e in range(2):
            part = latent_t[:, e * rows : (e + 1) * rows].T
            done = dot_nn(part, uv_ref[i + e])
            out_ref[:, pl.ds((i + e) * value_width, value_width)] = done.astype(BF16)


def outputs(prompt_values, resp_latent, attention_t, own_weights, ratio, up_value):
    resp_count, key_span, columns = attention_t.shape
    channels = resp_latent.shape[1]
    heads, latent_width, value_width = up_value.shape
    rows = resp_latent.shape[0] // resp_count
    return pl.pallas_call(
        output_kernel,
        grid=(resp_count,),
        in_specs=[
            pl.BlockSpec((1, key_span, latent_width), lambda j: (j, 0, 0)),
            pl.BlockSpec((rows, channels), lambda j: (j, 0)),
            pl.BlockSpec((1, key_span, columns), lambda j: (j, 0, 0)),
            pl.BlockSpec((1, rows, columns), lambda j: (j, 0, 0)),
            pl.BlockSpec((1, 8, columns), lambda j: (j, 0, 0)),
            pl.BlockSpec((heads, latent_width, value_width), lambda j: (0, 0, 0)),
        ],
        out_specs=pl.BlockSpec((rows, heads * value_width), lambda j: (j, 0)),
        out_shape=jax.ShapeDtypeStruct((resp_count * rows, heads * value_width), BF16),
        compiler_params=pltpu.CompilerParams(vmem_limit_bytes=12*1024*1024),
        cost_estimate=pl.CostEstimate(
            flops=2 * resp_count * columns * (384 + 128) * 512,
            bytes_accessed=16 * 1024 * 1024,
            transcendentals=0,
        ),
        name="outputs",
    )(*in_hbm(prompt_values, resp_latent, attention_t, own_weights, ratio, up_value))


def on_device(
    queries, up_key, up_value, prompt_latent, resp_latent, grad_out, response_prompt, prompt_length
):
    extents = tuple(lax.axis_size(name) for name in ORDER)
    cores, _, _, width = extents
    groups = cores * width
    my_group = lax.axis_index(RESP)
    owned, slab_rows, channels = prompt_latent.shape
    resp_count = response_prompt.shape[0] // groups
    owners = response_prompt // owned
    hit_table = owners[:, None] == jnp.arange(groups)[None, :]
    wanted = jnp.max(
        jnp.where(hit_table, (response_prompt % owned)[:, None], -1).reshape(
            groups, resp_count, groups
        ),
        axis=1,
    )
    wanted_mine = lax.dynamic_index_in_dim(wanted, my_group, 1, False)
    copies = pack(response_prompt, prompt_latent, extents)
    arrived = lax.all_to_all(
        copies.reshape((-1,) + copies.shape[4:]), ORDER, split_axis=0, concat_axis=0, tiled=True
    )
    gathered = arrived.reshape(copies.shape)
    local_prompt = lax.dynamic_slice_in_dim(response_prompt, my_group * resp_count, resp_count)
    slots = local_prompt // owned
    hits = local_prompt[:, None] == jnp.arange(prompt_length.shape[0])[None, :]
    lengths = jnp.sum(jnp.where(hits, prompt_length[None, :], 0), axis=1)
    head_width = queries.shape[1] // up_key.shape[0]
    full_t, grad_t = lift_tokens(queries, up_key, grad_out, up_value, resp_count)
    own_weights, stats = own_scores(resp_latent, full_t, grad_t, head_width)
    attention_t, ratio, prompt_values, pieces = attend(
        slots, lengths, gathered, stats, full_t, grad_t, head_width
    )
    returned_grad = lax.all_to_all(
        pieces.reshape((-1,) + pieces.shape[4:]), ORDER, split_axis=0, concat_axis=0, tiled=True
    )
    attn_out = outputs(prompt_values, resp_latent, attention_t, own_weights, ratio, up_value)
    summed = jnp.sum(returned_grad.reshape(pieces.shape).astype(F32), axis=(1, 2))
    kept = wanted_mine.reshape(width, cores).T[:, :, None, None]
    packed = jnp.stack(
        [jnp.sum(jnp.where(kept == p, summed, 0.0), axis=(0, 1)) for p in range(owned)]
    )
    blocks = channels // 128
    latent = packed[:, : slab_rows * blocks].reshape(owned, blocks, slab_rows, 128)
    tail = packed[:, slab_rows * blocks :].reshape(owned, slab_rows // 2, 2, 64)
    prompt_grad = jnp.concatenate(
        [
            jnp.transpose(latent, (0, 2, 1, 3)).reshape(owned, slab_rows, blocks * 128),
            jnp.transpose(tail, (0, 2, 1, 3)).reshape(owned, slab_rows, 64),
        ],
        axis=2,
    )
    return (attn_out, prompt_grad)


def solution(mesh):
    groups, slab_count = mesh.devices.shape
    devices = mesh.devices.reshape(groups // 2, 2, slab_count // 4, 4)
    return jax.shard_map(
        on_device,
        mesh=Mesh(devices, RESP + HEAD),
        in_specs=(
            P(RESP, HEAD),
            P(HEAD, None, None),
            P(HEAD, None, None),
            P(RESP, HEAD, None),
            P(RESP, None),
            P(RESP, HEAD),
            P(),
            P(),
        ),
        out_specs=(P(RESP, HEAD), P(RESP, HEAD, None)),
        check_vma=False,
    )
```

```python
import functools
import math

import jax
import jax.numpy as jnp
from jax import lax
from jax.experimental import pallas as pl
from jax.experimental.pallas import tpu as pltpu
from jax.sharding import PartitionSpec as P

BF16 = jnp.bfloat16
F32 = jnp.float32
LOG2E = 1.4426950408889634


def in_hbm(*arrays):
    return [pltpu.with_memory_space_constraint(a, pltpu.HBM) for a in arrays]


def dot_nn(a, b):
    return lax.dot_general(a, b, (((1,), (0,)), ((), ())), preferred_element_type=F32)


def dot_nt(a, b):
    return lax.dot_general(a, b, (((1,), (1,)), ((), ())), preferred_element_type=F32)


def up_kernel(q_ref, uk_ref, go_ref, uv_ref, fq_ref, gl_ref):
    resp_count, channels, _ = fq_ref.shape
    latent_width = gl_ref.shape[1]
    rope = channels - latent_width
    rows = q_ref.shape[0] // resp_count
    nope = uk_ref.shape[1]
    span = 2 * nope
    for e in range(2):
        lead = e * rope
        lift = uk_ref[e]
        parts = [lift, jnp.zeros((nope - lead, latent_width), BF16)]
        if lead:
            parts = [jnp.zeros((lead, latent_width), BF16)] + parts
        lifted = jnp.concatenate(parts, axis=0).T
        row = lax.broadcasted_iota(jnp.int32, (rope, span), 0)
        col = lax.broadcasted_iota(jnp.int32, (rope, span), 1)
        pick = jnp.where(col == row + (nope + lead), 1.0, 0.0).astype(BF16)
        up_value = uv_ref[e]
        for j in range(0, resp_count, 2):
            window = q_ref[pl.ds(j * rows, 2 * rows), pl.ds(e * nope, span)]
            grad = go_ref[pl.ds(j * rows, 2 * rows), pl.ds(e * rows, rows)]
            top = dot_nt(lifted, window).astype(BF16)
            low = dot_nt(pick, window).astype(BF16)
            lat = dot_nt(up_value, grad).astype(BF16)
            for i in range(2):
                src = slice(i * rows, (i + 1) * rows)
                dst = pl.ds(e * rows, rows)
                fq_ref[j + i, pl.ds(0, latent_width), dst] = top[:, src]
                fq_ref[j + i, pl.ds(latent_width, rope), dst] = low[:, src]
                gl_ref[j + i, :, dst] = lat[:, src]


def lift_tokens(queries, up_key, grad_out, up_value, resp_count):
    tokens = queries.shape[0]
    rows = tokens // resp_count
    heads, nope, latent_width = up_key.shape
    value_width = up_value.shape[2]
    head_width = queries.shape[1] // heads
    channels = latent_width + head_width - nope
    return pl.pallas_call(
        up_kernel,
        grid=(heads // 2,),
        in_specs=[
            pl.BlockSpec((tokens, 2 * head_width), lambda i: (0, i)),
            pl.BlockSpec((2, nope, latent_width), lambda i: (i, 0, 0)),
            pl.BlockSpec((tokens, 2 * value_width), lambda i: (0, i)),
            pl.BlockSpec((2, latent_width, value_width), lambda i: (i, 0, 0)),
        ],
        out_specs=[
            pl.BlockSpec((resp_count, channels, 2 * rows), lambda i: (0, 0, i)),
            pl.BlockSpec((resp_count, latent_width, 2 * rows), lambda i: (0, 0, i)),
        ],
        out_shape=[
            pltpu.HBM((resp_count, channels, heads * rows), BF16),
            pltpu.HBM((resp_count, latent_width, heads * rows), BF16),
        ],
        compiler_params=pltpu.CompilerParams(vmem_limit_bytes=14*1024*1024),
        cost_estimate=pl.CostEstimate(
            flops=4 * tokens * heads * nope * latent_width,
            bytes_accessed=30 * 1024 * 1024,
            transcendentals=0,
        ),
        name="lift_tokens",
    )(*in_hbm(queries, up_key, grad_out, up_value))


def pack_rows(rows):
    slab, channels = rows.shape
    blocks = channels // 128
    half = slab // 2
    tail = jnp.concatenate([rows[:half, 128 * blocks :], rows[half:, 128 * blocks :]], axis=1)
    return jnp.concatenate([rows[:, 128 * c : 128 * (c + 1)] for c in range(blocks)] + [tail], axis=0)


def pack_kernel(axis, prompt_any, latent_any, out_ref, prompt_ref, latent_ref, sem):
    copies = [
        pltpu.make_async_copy(prompt_any, prompt_ref, sem.at[0]),
        pltpu.make_async_copy(latent_any, latent_ref, sem.at[1]),
    ]
    for copy in copies:
        copy.start()
    for copy in copies:
        copy.wait()
    groups, slab_count, packed_rows, lanes = out_ref.shape
    owned = latent_ref.shape[0]
    resp_count = prompt_ref.shape[0] // groups
    first = lax.axis_index(axis) * owned
    packed = [pack_rows(latent_ref[p].astype(F32)).astype(BF16) for p in range(owned)]
    for r in range(groups):
        chosen = packed[0]
        for p in range(1, owned):
            hits = [prompt_ref[r * resp_count + i] == first + p for i in range(resp_count)]
            chosen = jnp.where(functools.reduce(jnp.logical_or, hits), packed[p], chosen)
        out_ref[r] = jnp.broadcast_to(chosen[None], (slab_count, packed_rows, lanes))


def pack(response_prompt, prompt_latent, groups, slab_count):
    owned, slab_rows, channels = prompt_latent.shape
    packed_rows = slab_rows * channels // 128
    return pl.pallas_call(
        functools.partial(pack_kernel, "resp"),
        in_specs=[pl.BlockSpec(memory_space=pl.ANY)] * 2,
        out_specs=pl.BlockSpec(memory_space=pltpu.VMEM),
        scratch_shapes=[
            pltpu.SMEM(response_prompt.shape, response_prompt.dtype),
            pltpu.VMEM(prompt_latent.shape, BF16),
            pltpu.SemaphoreType.DMA((2,)),
        ],
        out_shape=pltpu.VMEM((groups, slab_count, packed_rows, 128), BF16),
        compiler_params=pltpu.CompilerParams(vmem_limit_bytes=10 * 1024 * 1024),
        name="pack",
    )(*in_hbm(response_prompt, prompt_latent))


def own_kernel(head_width, own_ref, fq_ref, gl_ref, e_ref, stat_ref):
    rows = own_ref.shape[0]
    latent_width = gl_ref.shape[1]
    columns = fq_ref.shape[2]
    scaling = LOG2E / math.sqrt(head_width)
    chunk = 2 * rows
    keys = own_ref[...]
    values = keys[:, :latent_width]
    row = lax.broadcasted_iota(jnp.int32, (rows, chunk), 0)
    col = lax.broadcasted_iota(jnp.int32, (rows, chunk), 1) % rows
    allowed = row <= col
    for c in range(columns // chunk):
        at = pl.ds(c * chunk, chunk)
        scores = dot_nn(keys, fq_ref[0, :, at])
        grad_att = dot_nn(values, gl_ref[0, :, at])
        scores = jnp.where(allowed, scores * scaling, -1e30)
        top = jnp.max(scores, axis=0, keepdims=True)
        weights = jnp.exp2(scores - top)
        e_ref[0, :, at] = weights.astype(BF16)
        stat_ref[0, pl.ds(0, 1), at] = top
        stat_ref[0, pl.ds(1, 1), at] = jnp.sum(weights, axis=0, keepdims=True)
        stat_ref[0, pl.ds(2, 1), at] = jnp.sum(weights * grad_att, axis=0, keepdims=True)


def own_scores(resp_latent, full_t, grad_t, head_width):
    resp_count, channels, columns = full_t.shape
    latent_width = grad_t.shape[1]
    rows = resp_latent.shape[0] // resp_count
    return pl.pallas_call(
        functools.partial(own_kernel, head_width),
        grid=(resp_count,),
        in_specs=[
            pl.BlockSpec((rows, channels), lambda j: (j, 0)),
            pl.BlockSpec((1, channels, columns), lambda j: (j, 0, 0)),
            pl.BlockSpec((1, latent_width, columns), lambda j: (j, 0, 0)),
        ],
        out_specs=[
            pl.BlockSpec((1, rows, columns), lambda j: (j, 0, 0)),
            pl.BlockSpec((1, 8, columns), lambda j: (j, 0, 0)),
        ],
        out_shape=[
            pltpu.HBM((resp_count, rows, columns), BF16),
            pltpu.HBM((resp_count, 8, columns), F32),
        ],
        compiler_params=pltpu.CompilerParams(vmem_limit_bytes=10*1024*1024),
        cost_estimate=pl.CostEstimate(
            flops=2 * resp_count * columns * rows * (channels + latent_width),
            bytes_accessed=22 * 1024 * 1024,
            transcendentals=resp_count * columns * rows,
        ),
        name="own_scores",
    )(*in_hbm(resp_latent, full_t, grad_t))


def unpack_latent(packed_ref, slab):
    slabs, packed_rows, lanes = packed_ref.shape[1:]
    return jnp.concatenate(
        [
            jnp.concatenate(
                [packed_ref[0, h, pl.ds(slab * c, slab), :] for h in range(slabs)], axis=0
            )
            for c in range(packed_rows // slab)
        ],
        axis=1,
    )


def unpack_rope(packed_ref, slab):
    slabs, packed_rows, lanes = packed_ref.shape[1:]
    rows = []
    for h in range(slabs):
        tail = packed_ref[0, h].astype(F32)[packed_rows - slab // 2 :]
        rows += [tail[:, : lanes // 2], tail[:, lanes // 2 :]]
    return jnp.concatenate(rows, axis=0).astype(BF16)


def attend_kernel(
    head_width,
    slot_ref,
    len_ref,
    latent_ref,
    stat_ref,
    fq_ref,
    gl_ref,
    aT_ref,
    ratio_ref,
    value_ref,
    piece_ref,
    acc_ref,
    gs_ref,
):
    j = pl.program_id(0)
    channels = fq_ref.shape[1]
    latent_width = gl_ref.shape[1]
    columns = fq_ref.shape[2]
    rope = channels - latent_width
    groups, key_span, _ = acc_ref.shape
    slabs = latent_ref.shape[1]
    slab = key_span // slabs
    scaling = 1.0 / math.sqrt(head_width)
    chunk = 256

    slot = slot_ref[j]
    length = len_ref[j]
    seen = jnp.int32(0)
    for k in range(slot_ref.shape[0]):
        seen = jnp.where((k < j) & (slot_ref[k] == slot), 1, seen)
    values = unpack_latent(latent_ref, slab)
    value_ref[0] = values
    keys_rope = unpack_rope(latent_ref, slab)
    row = lax.broadcasted_iota(jnp.int32, (key_span, chunk), 0)
    allowed = row < length
    for c in range(columns // chunk):
        at = pl.ds(c * chunk, chunk)
        both = jnp.concatenate([fq_ref[0, pl.ds(0, latent_width), at], gl_ref[0, :, at]], axis=1)
        both = dot_nn(values, both)
        rotary = dot_nn(keys_rope, fq_ref[0, pl.ds(latent_width, rope), at])
        scores = both[:, :chunk] + rotary
        grad_att = both[:, chunk:]
        own_top = stat_ref[0, pl.ds(0, 1), at]
        scores = jnp.where(allowed, scores * (scaling * LOG2E), -1e30)
        top = jnp.maximum(jnp.max(scores, axis=0, keepdims=True), own_top)
        weights = jnp.exp2(scores - top)
        shift = jnp.exp2(own_top - top)
        total = jnp.sum(weights, axis=0, keepdims=True) + shift * stat_ref[0, pl.ds(1, 1), at]
        inverse = 1.0 / total
        inner = jnp.sum(weights * grad_att, axis=0, keepdims=True)
        inner = (inner + shift * stat_ref[0, pl.ds(2, 1), at]) * inverse
        gs_ref[:, at] = (weights * (grad_att - inner) * (inverse * scaling)).astype(BF16)
        aT_ref[0, :, at] = (weights * inverse).astype(BF16)
        ratio_ref[0, pl.ds(0, 1), at] = shift * inverse
    combined = dot_nt(gs_ref[...], fq_ref[0])
    value_term = dot_nt(aT_ref[0], gl_ref[0])
    latent_part = combined[:, :latent_width] + value_term
    rope_part = combined[:, latent_width:]
    earlier = acc_ref[slot]
    latent_part += jnp.where(seen == 1, earlier[:, :latent_width], 0.0)
    rope_part += jnp.where(seen == 1, earlier[:, latent_width:], 0.0)
    acc_ref[slot, :, pl.ds(0, latent_width)] = latent_part
    acc_ref[slot, :, pl.ds(latent_width, rope)] = rope_part
    total = jnp.concatenate([latent_part, rope_part], axis=1)
    for h in range(slabs):
        piece_ref[0, h] = pack_rows(total[h * slab : (h + 1) * slab]).astype(BF16)


def attend(slots, lengths, gathered, stats, full_t, grad_t, head_width):
    groups, slabs, packed_rows, lanes = gathered.shape
    resp_count, channels, columns = full_t.shape
    key_span = slabs * packed_rows * lanes // channels
    latent_width = grad_t.shape[1]
    grid_spec = pltpu.PrefetchScalarGridSpec(
        num_scalar_prefetch=2,
        grid=(resp_count,),
        in_specs=[
            pl.BlockSpec((1, slabs, packed_rows, lanes), lambda j, s, n: (s[j], 0, 0, 0)),
            pl.BlockSpec((1, 8, columns), lambda j, s, n: (j, 0, 0)),
            pl.BlockSpec((1, channels, columns), lambda j, s, n: (j, 0, 0)),
            pl.BlockSpec((1, latent_width, columns), lambda j, s, n: (j, 0, 0)),
        ],
        out_specs=[
            pl.BlockSpec((1, key_span, columns), lambda j, s, n: (j, 0, 0)),
            pl.BlockSpec((1, 8, columns), lambda j, s, n: (j, 0, 0)),
            pl.BlockSpec((1, key_span, latent_width), lambda j, s, n: (j, 0, 0)),
            pl.BlockSpec((1, slabs, packed_rows, lanes), lambda j, s, n: (s[j], 0, 0, 0)),
        ],
        scratch_shapes=[
            pltpu.VMEM((groups, key_span, channels), F32),
            pltpu.VMEM((key_span, columns), BF16),
        ],
    )
    return pl.pallas_call(
        functools.partial(attend_kernel, head_width),
        grid_spec=grid_spec,
        out_shape=[
            pltpu.HBM((resp_count, key_span, columns), BF16),
            pltpu.HBM((resp_count, 8, columns), F32),
            pltpu.HBM((resp_count, key_span, latent_width), BF16),
            pltpu.HBM((groups, slabs, packed_rows, lanes), BF16),
        ],
        compiler_params=pltpu.CompilerParams(vmem_limit_bytes=20*1024*1024),
        cost_estimate=pl.CostEstimate(
            flops=2 * resp_count * columns * key_span * 2176,
            bytes_accessed=30 * 1024 * 1024,
            transcendentals=resp_count * columns * key_span,
        ),
        name="attend",
    )(slots, lengths, gathered, *in_hbm(stats, full_t, grad_t))


def output_kernel(latent_ref, own_ref, aT_ref, e_ref, ratio_ref, uv_ref, out_ref):
    rows = own_ref.shape[0]
    heads, latent_width, value_width = uv_ref.shape
    values = jnp.concatenate(
        [latent_ref[0], own_ref[:, pl.ds(0, latent_width)]], axis=0
    )
    values_t = values.T
    for i in range(0, heads, 2):
        at = pl.ds(i * rows, 2 * rows)
        own = (e_ref[0, :, at].astype(F32) * ratio_ref[0, pl.ds(0, 1), at]).astype(BF16)
        weights = jnp.concatenate([aT_ref[0, :, at], own], axis=0)
        latent_t = dot_nn(values_t, weights).astype(BF16)
        for e in range(2):
            part = latent_t[:, e * rows : (e + 1) * rows].T
            done = dot_nn(part, uv_ref[i + e])
            out_ref[:, pl.ds((i + e) * value_width, value_width)] = done.astype(BF16)


def outputs(prompt_values, resp_latent, attention_t, own_weights, ratio, up_value):
    resp_count, key_span, columns = attention_t.shape
    channels = resp_latent.shape[1]
    heads, latent_width, value_width = up_value.shape
    rows = resp_latent.shape[0] // resp_count
    return pl.pallas_call(
        output_kernel,
        grid=(resp_count,),
        in_specs=[
            pl.BlockSpec((1, key_span, latent_width), lambda j: (j, 0, 0)),
            pl.BlockSpec((rows, channels), lambda j: (j, 0)),
            pl.BlockSpec((1, key_span, columns), lambda j: (j, 0, 0)),
            pl.BlockSpec((1, rows, columns), lambda j: (j, 0, 0)),
            pl.BlockSpec((1, 8, columns), lambda j: (j, 0, 0)),
            pl.BlockSpec((heads, latent_width, value_width), lambda j: (0, 0, 0)),
        ],
        out_specs=pl.BlockSpec((rows, heads * value_width), lambda j: (j, 0)),
        out_shape=jax.ShapeDtypeStruct((resp_count * rows, heads * value_width), BF16),
        compiler_params=pltpu.CompilerParams(vmem_limit_bytes=12*1024*1024),
        cost_estimate=pl.CostEstimate(
            flops=2 * resp_count * columns * (384 + 128) * 512,
            bytes_accessed=16 * 1024 * 1024,
            transcendentals=0,
        ),
        name="outputs",
    )(*in_hbm(prompt_values, resp_latent, attention_t, own_weights, ratio, up_value))


def on_device(
    queries, up_key, up_value, prompt_latent, resp_latent, grad_out, response_prompt, prompt_length
):
    groups = lax.axis_size("resp")
    slab_count = lax.axis_size("head")
    my_group = lax.axis_index("resp")
    owned, slab_rows, channels = prompt_latent.shape
    resp_count = response_prompt.shape[0] // groups
    owners = response_prompt // owned
    hit_table = owners[:, None] == jnp.arange(groups)[None, :]
    wanted = jnp.max(
        jnp.where(hit_table, (response_prompt % owned)[:, None], -1).reshape(
            groups, resp_count, groups
        ),
        axis=1,
    )
    wanted_mine = lax.dynamic_index_in_dim(wanted, my_group, 1, False)
    copies = pack(response_prompt, prompt_latent, groups, slab_count)
    copies = copies.reshape(groups * slab_count, -1, 128)
    arrived = lax.all_to_all(copies, ("resp", "head"), split_axis=0, concat_axis=0, tiled=True)
    gathered = arrived.reshape(groups, slab_count, -1, 128)
    local_prompt = lax.dynamic_slice_in_dim(response_prompt, my_group * resp_count, resp_count)
    slots = local_prompt // owned
    hits = local_prompt[:, None] == jnp.arange(prompt_length.shape[0])[None, :]
    lengths = jnp.sum(jnp.where(hits, prompt_length[None, :], 0), axis=1)
    head_width = queries.shape[1] // up_key.shape[0]
    full_t, grad_t = lift_tokens(queries, up_key, grad_out, up_value, resp_count)
    own_weights, stats = own_scores(resp_latent, full_t, grad_t, head_width)
    attention_t, ratio, prompt_values, pieces = attend(
        slots, lengths, gathered, stats, full_t, grad_t, head_width
    )
    returned_grad = lax.all_to_all(
        pieces.reshape(groups * slab_count, -1, 128),
        ("resp", "head"),
        split_axis=0,
        concat_axis=0,
        tiled=True,
    )
    attn_out = outputs(prompt_values, resp_latent, attention_t, own_weights, ratio, up_value)
    summed = jnp.sum(returned_grad.reshape(groups, slab_count, -1, 128).astype(F32), axis=1)
    packed = jnp.stack(
        [
            jnp.sum(jnp.where((wanted_mine == p)[:, None, None], summed, 0.0), axis=0)
            for p in range(owned)
        ]
    )
    blocks = channels // 128
    latent = packed[:, : slab_rows * blocks].reshape(owned, blocks, slab_rows, 128)
    tail = packed[:, slab_rows * blocks :].reshape(owned, slab_rows // 2, 2, 64)
    prompt_grad = jnp.concatenate(
        [
            jnp.transpose(latent, (0, 2, 1, 3)).reshape(owned, slab_rows, blocks * 128),
            jnp.transpose(tail, (0, 2, 1, 3)).reshape(owned, slab_rows, 64),
        ],
        axis=2,
    )
    return (attn_out, prompt_grad)


def solution(mesh):
    return jax.shard_map(
        on_device,
        mesh=mesh,
        in_specs=(
            P("resp", "head"),
            P("head", None, None),
            P("head", None, None),
            P("resp", "head", None),
            P("resp", None),
            P("resp", "head"),
            P(),
            P(),
        ),
        out_specs=(P("resp", "head"), P("resp", "head", None)),
        check_vma=False,
    )
```
